512 devices in a mesh: section: 4 (over z_hi), dp: 16 (over y, z_lo), expert: 8 (over x, core).
Axes of the slice: x: 4, y: 4, z: 16 (z_hi: 4, z_lo: 4; z = z_hi * 4 + z_lo), core: 2. Of those that a mesh axis runs over, the one named last changes fastest.
Arguments:
- normed: bfloat16 [4, 2048, 3584], P('section', 'dp'), may hold values from -6 to 6
- residual: bfloat16 [4, 2048, 3584], P('section', 'dp', 'expert'), may hold values from -6 to 6
- expert_index: int32 [4, 2048, 2], P('section', 'dp'), may hold values from 0 to 7, all different within a row; in each aligned block of 128 rows (0 to 127, 128 to 255, ..., all dimensions but the last counted through in order) at most 36 rows name the same one
- pick_weight: float32 [4, 2048, 2], P('section', 'dp'), may hold values from 0.25 to 1
- dense_gate: bfloat16 [4, 3584, 3072], P('section', 'dp', 'expert'), may hold values from -0.09375 to 0.09375
- dense_up: bfloat16 [4, 3584, 3072], P('section', 'dp', 'expert'), may hold values from -0.09375 to 0.09375
- dense_down: bfloat16 [4, 3584, 3072], P('section', 'dp', 'expert'), may hold values from -0.109375 to 0.109375
- expert_gate: bfloat16 [4, 8, 3584, 2432], P('section', 'expert', None, 'dp'), may hold values from -0.09375 to 0.09375
- expert_up: bfloat16 [4, 8, 3584, 2432], P('section', 'expert', None, 'dp'), may hold values from -0.09375 to 0.09375
- expert_down: bfloat16 [4, 8, 2432, 3584], P('section', 'expert', 'dp'), may hold values from -0.125 to 0.125
Outputs:
- layer_out: bfloat16 [4, 2048, 3584], P('section', 'dp', 'expert')
The draws below stay inside these ranges and needn't reach their ends.
Inputs may be any that keep to these rules, and one draw needn't show every extreme that they name: `expert_index`: each row names 2 different experts. Among the 128 tokens of one block no expert is named by more than 36 of them, and in every draw some expert is named by exactly 36 tokens of some block.
All inputs are finite; a program needn't handle non-finite values.
Results may differ from the reference program's by a relative error of at most 0.0051.
Values may be sent and summed in bfloat16 or wider, within the bound.
No kernel may reach another device: no remote copies, remote signals or barrier semaphores. Data moves between devices by JAX's collectives and lax.ppermute only.
A program may use at most 64 MiB of HBM per device.

```python
import math
import jax
import jax.numpy as jnp
import numpy as np
from jax import lax

D = 3584
FE = 2432
FD = 3072
TOK = 128
TOP = 2
SECTIONS = 4
EXPERTS = 8
TOKENS = 2048
CAP = 36
HBLK = 152
DBLK = 384


def steps_of(key, extent, shards, smallest, largest):
    gain, own = 1.0, jax.random.fold_in(key, 6)
    for axis_at, shards_of in shards:
        steps = jnp.exp(jax.random.uniform(jax.random.fold_in(own, axis_at), (shards_of,), jnp.float32, smallest / len(shards), largest / len(shards)))
        gain = gain * jnp.repeat(steps, extent[axis_at] // shards_of).reshape([-1 if axis == axis_at else 1 for axis in range(len(extent))])
    return gain


def assign_block(key, own, number, rows, count, top, reach, skew):
    sequence = jax.random.permutation(key, count)
    crowded, usual = load_shares(count, rows * top, reach, skew, True), load_shares(count, rows * top, reach, skew, False)
    places = jnp.arange(count)

    def named(sizes, offset_by):
        used = int((sizes > 0).sum())
        fixed = max(1, used // 4)
        shifted = fixed + (places - fixed + offset_by * (used - fixed)) % max(1, count - fixed)
        return jnp.zeros((count,), jnp.int32).at[sequence[jnp.where(places < fixed, places, shifted)]].set(jnp.asarray(sizes, jnp.int32))

    sizes = jnp.where(number % 4 == 0, named(crowded, number // 4), named(usual, number - number // 4 - 1))
    mixed = jax.random.permutation(jax.random.fold_in(own, 3), count)
    source_of, receiver = mixed[0:count // 2 * 2:2], mixed[1:count // 2 * 2:2]
    margin = jnp.minimum(sizes[source_of] - 1, reach - sizes[receiver]) // 2
    margin = jnp.where((source_of == sequence[0]) | (receiver == sequence[0]) | (sizes[receiver] == 0), 0, jnp.maximum(margin, 0))
    shifted = jax.random.randint(jax.random.fold_in(own, 4), (count // 2,), 0, 1 << 20) % (margin + 1)
    sizes = sizes.at[source_of].add(-shifted).at[receiver].add(shifted)
    items = jnp.searchsorted(jnp.cumsum(sizes), jnp.arange(rows * top), side="right").astype(jnp.int32)
    grid = items.reshape(top, rows).T
    grid = grid[jax.random.permutation(jax.random.fold_in(own, 1), rows)]
    offset_by = jax.random.randint(jax.random.fold_in(own, 2), (rows, 1), 0, top)
    return jnp.take_along_axis(grid, (jnp.arange(top)[None, :] + offset_by) % top, axis=1)


def load_shares(number_of, total, bound, slope, full):
    portions = [(1 << 20) // math.isqrt(rank ** slope) + 1 for rank in range(1, number_of + 1)]
    largest = bound if full else min(bound, max(-(-total // number_of), total * portions[0] // sum(portions)))
    least = 1 if total - largest >= number_of - 1 else 0
    given, surplus = [largest] + [least] * (number_of - 1), total - largest - least * (number_of - 1)
    while surplus > 0:
        free = [i for i in range(1, number_of) if given[i] < largest] or [i for i in range(1, number_of) if given[i] < bound]
        pool, left = sum([portions[i] for i in free]), surplus
        for i in free:
            more = min(bound - given[i], max(1, left * portions[i] // pool), surplus)
            given[i] = given[i] + more
            surplus = surplus - more
    return np.array(given)


def gaussian(stream_key, extent, spread, reach, pieces=(), held_as=jnp.bfloat16):
    values = spread * jax.random.normal(stream_key, extent, jnp.float32)
    if pieces:
        values = values * steps_of(stream_key, extent, pieces, -0.22, 0.18)
    return jnp.clip(values, -reach, reach).astype(held_as)


def setup_inputs(seed: int = 0) -> dict:
    key_list = jax.random.split(jax.random.key(seed), 11)
    normed = gaussian(key_list[0], (SECTIONS, TOKENS, D), 1.0, 6.0, ((0, 4), (1, 16)))
    residual = gaussian(key_list[1], (SECTIONS, TOKENS, D), 1.0, 6.0, ((0, 4), (1, 16), (2, 8)))
    expert_index_keys = jax.random.split(jax.random.fold_in(key_list[2], 1), SECTIONS * TOKENS // TOK)
    expert_index_turns = jax.random.permutation(jax.random.fold_in(key_list[2], 3), SECTIONS * TOKENS // TOK)
    expert_index = jax.vmap(lambda own, number: assign_block(jax.random.fold_in(key_list[2], 2), own, number, TOK, EXPERTS, TOP, CAP, 1))(expert_index_keys, expert_index_turns).reshape((SECTIONS, TOKENS, TOP))
    pick_weight = jnp.clip(0.25 + 0.75 * jax.random.uniform(key_list[3], (SECTIONS, TOKENS, TOP), jnp.float32) ** steps_of(key_list[3], (SECTIONS, TOKENS, TOP), ((0, 4), (1, 16)), -0.2, 0.2), 0.25, 1.0)
    dense_gate = gaussian(key_list[4], (SECTIONS, D, FD), D ** -0.5, 0.09375, ((0, 4), (1, 16), (2, 8)))
    dense_up = gaussian(key_list[5], (SECTIONS, D, FD), D ** -0.5, 0.09375, ((0, 4), (1, 16), (2, 8)))
    dense_down = gaussian(key_list[6], (SECTIONS, D, FD), FD ** -0.5, 0.109375, ((0, 4), (1, 16), (2, 8)))
    expert_gate = gaussian(key_list[7], (SECTIONS, EXPERTS, D, FE), D ** -0.5, 0.09375, ((0, 4), (1, 8), (3, 16)))
    expert_up = gaussian(key_list[8], (SECTIONS, EXPERTS, D, FE), D ** -0.5, 0.09375, ((0, 4), (1, 8), (3, 16)))
    expert_down = gaussian(key_list[9], (SECTIONS, EXPERTS, FE, D), FE ** -0.5, 0.125, ((0, 4), (1, 8), (2, 16)))
    return dict(normed=normed, residual=residual, expert_index=expert_index, pick_weight=pick_weight, dense_gate=dense_gate, dense_up=dense_up, dense_down=dense_down, expert_gate=expert_gate, expert_up=expert_up, expert_down=expert_down)


def swiglu(first, second):
    return (jax.nn.silu(first) * second).astype(jnp.bfloat16)


def rounded(value):
    return lax.optimization_barrier(value.astype(jnp.bfloat16)).astype(jnp.float32)


def slots_of(picks):
    labels = jnp.arange(EXPERTS, dtype=jnp.int32)
    named = (picks[:, :, None] == labels[None, None, :]).astype(jnp.int32)
    per_token = jnp.sum(named, axis=1, dtype=jnp.int32).reshape(TOKENS // TOK, TOK, EXPERTS)
    earlier = jnp.cumsum(per_token, axis=1, dtype=jnp.int32) - per_token
    earlier = earlier.reshape(TOKENS, EXPERTS)
    return jnp.take_along_axis(earlier, picks, axis=1).astype(jnp.int32)


def section_layer(normed, residual, picks, weights, dense_gate, dense_up, dense_down, expert_gate, expert_up, expert_down):
    contract = (((1,), (1,)), ((), ()))
    dense_hidden = swiglu(jnp.dot(normed, dense_gate, preferred_element_type=jnp.float32),
                          jnp.dot(normed, dense_up, preferred_element_type=jnp.float32))
    dense_sum = jnp.zeros((TOKENS, D), jnp.float32)
    for block in range(FD // DBLK):
        piece = dense_hidden[:, block * DBLK:(block + 1) * DBLK]
        columns = dense_down[:, block * DBLK:(block + 1) * DBLK]
        term = lax.dot_general(piece, columns, contract, preferred_element_type=jnp.float32)
        dense_sum = dense_sum + rounded(term)
    slot = slots_of(picks)
    owner = (jnp.arange(TOKENS, dtype=jnp.int32) // TOK)[:, None] + jnp.zeros_like(picks)
    source = jnp.broadcast_to(normed[:, None, :], (TOKENS, TOP, D))
    dispatched = jnp.zeros((EXPERTS, TOKENS // TOK, CAP, D), jnp.bfloat16).at[picks, owner, slot].set(source)
    produced = []
    for expert in range(EXPERTS):
        rows = dispatched[expert].reshape((TOKENS // TOK) * CAP, D)
        hidden = swiglu(jnp.dot(rows, expert_gate[expert], preferred_element_type=jnp.float32),
                        jnp.dot(rows, expert_up[expert], preferred_element_type=jnp.float32))
        total = jnp.zeros(((TOKENS // TOK) * CAP, D), jnp.float32)
        for block in range(FE // HBLK):
            term = jnp.dot(hidden[:, block * HBLK:(block + 1) * HBLK],
                           expert_down[expert, block * HBLK:(block + 1) * HBLK],
                           preferred_element_type=jnp.float32)
            total = total + rounded(term)
        produced.append(total.astype(jnp.bfloat16).reshape(TOKENS // TOK, CAP, D))
    outputs = jnp.stack(produced)
    picked = outputs[picks, owner, slot].astype(jnp.float32)
    mixed = residual.astype(jnp.float32) + dense_sum + jnp.sum(weights[:, :, None] * picked, axis=1)
    return mixed.astype(jnp.bfloat16)


def reference(normed, residual, expert_index, pick_weight, dense_gate, dense_up, dense_down, expert_gate, expert_up, expert_down):
    results = []
    for section in range(SECTIONS):
        results.append(section_layer(normed[section], residual[section], expert_index[section], pick_weight[section],
                                   dense_gate[section], dense_up[section], dense_down[section],
                                   expert_gate[section], expert_up[section], expert_down[section]))
    mixed = jnp.stack(results)
    return jnp.roll(mixed, 1, axis=0)
```

```python
import jax
import jax.numpy as jnp
from jax import lax
from jax.sharding import Mesh, PartitionSpec as P

AXES = ("section", "y", "z", "x", "core")
GRID = (4, 4, 4, 4, 2)
EXPERT_AXES = ("x", "core")


def shifted(x, axis, by):
    peers = lax.axis_size(axis)
    return lax.ppermute(x, axis, [(i, (i + by) % peers) for i in range(peers)])


def exchanged(x, axes):
    return lax.all_to_all(x, axes, split_axis=0, concat_axis=0, tiled=True)


def swiglu(first, second):
    return (jax.nn.silu(first) * second).astype(jnp.bfloat16)


def dot(a, b):
    return jnp.dot(a, b, preferred_element_type=jnp.float32)


def slots_of(picks, n_expert):
    labels = jnp.arange(n_expert, dtype=jnp.int32)
    named = (picks[:, :, None] == labels[None, None, :]).astype(jnp.int32)
    per_token = jnp.sum(named, axis=1, dtype=jnp.int32)
    earlier = jnp.cumsum(per_token, axis=0, dtype=jnp.int32) - per_token
    return jnp.sum(named * earlier[:, None, :], axis=2, dtype=jnp.int32)


def gathered_line(x, axis):
    mine = lax.axis_index(axis)
    parts = [x] + [shifted(x, axis, by) for by in (1, 2, 3)]
    stacked = jnp.stack(parts)
    order = (mine - jnp.arange(4, dtype=jnp.int32)) % 4
    return jnp.take(stacked, order, axis=0)


def body(
    normed,
    residual,
    expert_index,
    pick_weight,
    dense_gate,
    dense_up,
    dense_down,
    expert_gate,
    expert_up,
    expert_down,
):
    bf16, f32 = jnp.bfloat16, jnp.float32
    tokens = normed[0]
    picks = expert_index[0]
    weights = pick_weight[0]
    tok_rows, width = tokens.shape
    n_expert = 8
    capacity = min(tok_rows, 9 * tok_rows // (4 * n_expert))
    core = lax.axis_index("core")
    mine = lax.axis_index("x") * 2 + core
    hidden = dense_gate.shape[2]
    slab = width // 4
    step = dense_gate.shape[1]
    piece = width // n_expert

    stacked = jnp.concatenate([dense_gate[0], dense_up[0], dense_down[0]], axis=0)
    slabs = lax.all_gather(stacked, "y", axis=0, tiled=True).reshape(4, 3, step, hidden)
    gate_slab, up_slab, down_slab = (slabs[:, i].reshape(slab, hidden) for i in range(3))

    slot = slots_of(picks, n_expert)
    is_mine = picks == mine
    positions = jnp.arange(capacity, dtype=jnp.int32)
    select = jnp.any(
        (positions[:, None, None] == slot[None, :, :]) & is_mine[None, :, :], axis=2
    ).astype(bf16)
    routed = dot(select, tokens).astype(bf16)
    group = gathered_line(routed, "z").reshape(4 * capacity, width)

    packed = jnp.concatenate([picks * 128 + slot, jnp.zeros_like(picks)], axis=1)
    line_picks = lax.all_gather(packed[:, :2], "z", axis=0, tiled=True)
    line_weights = lax.all_gather(weights, "z", axis=0, tiled=True)

    gate_up = jnp.concatenate([expert_gate[0, 0], expert_up[0, 0]], axis=1)
    down = expert_down[0, 0]
    inner = down.shape[0]

    def ffn(rows):
        both = dot(rows, gate_up)
        return dot(swiglu(both[:, :inner], both[:, inner:]), down)

    half = 2 * capacity
    from_prev, from_next = shifted(group, "y", 1), shifted(group, "y", -1)
    far_low, far_high = shifted(from_prev[:half], "y", 1), shifted(from_next[half:], "y", -1)
    own_part = ffn(group)
    prev_part = ffn(from_prev)
    next_part = ffn(from_next)
    far_part = ffn(jnp.concatenate([far_low, far_high], axis=0)).astype(bf16)
    relay_next = shifted(far_part[:half], "y", 1)
    relay_prev = shifted(far_part[half:], "y", -1)
    to_next = jnp.concatenate(
        [next_part[:half] + relay_next.astype(f32), next_part[half:]], axis=0
    ).astype(bf16)
    to_prev = jnp.concatenate(
        [prev_part[:half], prev_part[half:] + relay_prev.astype(f32)], axis=0
    ).astype(bf16)
    back_a, back_b = shifted(to_next, "y", 1), shifted(to_prev, "y", -1)
    summed = (own_part + back_a.astype(f32) + back_b.astype(f32)).astype(bf16)

    half_tokens = tok_rows // 2
    by_line = tokens.reshape(tok_rows, 4, 4, step).transpose(2, 0, 1, 3).reshape(4, tok_rows, slab)
    own_half = lax.dynamic_slice_in_dim(by_line, core * half_tokens, half_tokens, axis=1)
    half_in = exchanged(own_half, "z")
    other_half = shifted(half_in, "core", 1)
    low = jnp.where(core == 0, half_in, other_half)
    high = jnp.where(core == 0, other_half, half_in)
    line_tokens = jnp.concatenate([low, high], axis=1).reshape(4 * tok_rows, slab)
    pre = jnp.concatenate([dot(line_tokens, gate_slab), dot(line_tokens, up_slab)], axis=1)
    pre = exchanged(pre.astype(bf16).reshape(4, tok_rows, 2 * hidden), "z")
    pre = jnp.sum(pre.astype(f32), axis=0)
    act = swiglu(pre[:, :hidden], pre[:, hidden:])
    line_act = gathered_line(act, "z").reshape(4 * tok_rows, hidden)
    contract = (((1,), (1,)), ((), ()))
    dense_out = lax.dot_general(line_act, down_slab, contract, preferred_element_type=f32)
    dense_in = exchanged(dense_out.astype(bf16).reshape(4, tok_rows, slab), "z")
    by_owner = (
        dense_in.reshape(2, 2, tok_rows, 4, step)
        .transpose(3, 0, 2, 1, 4)
        .reshape(n_expert, tok_rows, piece)
    )
    dense_total = jnp.sum(exchanged(by_owner, EXPERT_AXES).astype(f32), axis=0)
    base = residual[0].astype(f32) + dense_total

    by_feature = summed.reshape(4 * capacity, n_expert, piece).transpose(1, 0, 2)
    returned = exchanged(by_feature, EXPERT_AXES).reshape(n_expert * 4 * capacity, piece)
    line_expert, line_slot = line_picks // 128, line_picks % 128
    block = (jnp.arange(4 * tok_rows, dtype=jnp.int32) // tok_rows)[:, None]
    target = line_expert * (4 * capacity) + block * capacity + line_slot
    columns = jnp.arange(n_expert * 4 * capacity, dtype=jnp.int32)
    combine = jnp.sum(
        jnp.where(columns[None, None, :] == target[:, :, None], line_weights[:, :, None], 0.0),
        axis=1,
    )
    coarse = combine.astype(bf16)
    fine = (combine - coarse.astype(f32)).astype(bf16)
    mixed_part = (dot(coarse, returned) + dot(fine, returned)).astype(bf16)
    arrived = exchanged(mixed_part.reshape(4, tok_rows, piece), "z")
    mixed = (base + jnp.sum(arrived.astype(f32), axis=0)).astype(bf16)
    return shifted(mixed, "section", 1)[None]


def solution(mesh):
    fine_mesh = Mesh(mesh.devices.reshape(GRID), AXES)
    data = ("y", "z")
    placed = (
        P("section", data, None),
        P("section", data, EXPERT_AXES),
        P("section", data, None),
        P("section", data, None),
        P("section", data, EXPERT_AXES),
        P("section", data, EXPERT_AXES),
        P("section", data, EXPERT_AXES),
        P("section", EXPERT_AXES, None, data),
        P("section", EXPERT_AXES, None, data),
        P("section", EXPERT_AXES, data, None),
    )
    return jax.shard_map(
        body,
        mesh=fine_mesh,
        in_specs=placed,
        out_specs=P("section", data, EXPERT_AXES),
        check_vma=False,
    )
```

```python
import jax
import jax.numpy as jnp
from jax import lax
from jax.sharding import Mesh, PartitionSpec as P

AXES = ("section", "y", "z", "x", "core")
GRID = (4, 4, 4, 4, 2)
EXPERT_AXES = ("x", "core")
BF16, F32 = jnp.bfloat16, jnp.float32


def shifted(x, axis, by):
    peers = lax.axis_size(axis)
    return lax.ppermute(x, axis, [(i, (i + by) % peers) for i in range(peers)])


def exchanged(x, axes):
    return lax.all_to_all(x, axes, split_axis=0, concat_axis=0, tiled=True)


def after(x, *others):
    return lax.optimization_barrier((x,) + others)[0]


def swiglu(first, second):
    return (jax.nn.silu(first) * second).astype(BF16)


def dot(a, b):
    return jnp.dot(a, b, preferred_element_type=F32)


def slots_of(picks, n_expert):
    labels = jnp.arange(n_expert, dtype=jnp.int32)
    named = (picks[:, :, None] == labels[None, None, :]).astype(jnp.int32)
    per_token = jnp.sum(named, axis=1, dtype=jnp.int32)
    earlier = jnp.cumsum(per_token, axis=0, dtype=jnp.int32) - per_token
    return jnp.sum(named * earlier[:, None, :], axis=2, dtype=jnp.int32)


def body(
    normed,
    residual,
    expert_index,
    pick_weight,
    dense_gate,
    dense_up,
    dense_down,
    expert_gate,
    expert_up,
    expert_down,
):
    tokens = normed[0]
    picks = expert_index[0]
    weights = pick_weight[0]
    tok_rows, width = tokens.shape
    n_expert = 8
    capacity = min(tok_rows, 9 * tok_rows // (4 * n_expert))
    core = lax.axis_index("core")
    mine = lax.axis_index("x") * 2 + core
    hidden = dense_gate.shape[2]
    slab = width // 4
    step = dense_gate.shape[1]
    piece = width // n_expert

    with jax.named_scope("dense_weights"):
        stacked = jnp.concatenate([dense_gate[0], dense_up[0], dense_down[0]], axis=0)
        slabs = lax.all_gather(stacked, "y", axis=0, tiled=True)

    with jax.named_scope("dispatch"):
        slot = slots_of(picks, n_expert)
        is_mine = picks == mine
        positions = jnp.arange(capacity, dtype=jnp.int32)
        select = jnp.any(
            (positions[:, None, None] == slot[None, :, :]) & is_mine[None, :, :], axis=2
        ).astype(BF16)
        routed = dot(select, tokens).astype(BF16)

    with jax.named_scope("rows_z"):
        lines = [routed] + [shifted(routed, "z", by) for by in (1, 3, 2)]
        low = jnp.concatenate([lines[0], lines[1]], axis=0)
        high = jnp.concatenate([lines[2], lines[3]], axis=0)

    gate_up = jnp.concatenate([expert_gate[0, 0], expert_up[0, 0]], axis=1)
    down = expert_down[0, 0]
    inner = down.shape[0]

    def ffn(rows):
        both = dot(rows, gate_up)
        return dot(swiglu(both[:, :inner], both[:, inner:]), down)

    half = 2 * capacity
    with jax.named_scope("rows_y"):
        prev_low, next_low = shifted(low, "y", 1), shifted(low, "y", -1)
        far_low = shifted(prev_low, "y", 1)
        next_high, prev_high = shifted(high, "y", -1), shifted(high, "y", 1)
        far_high = shifted(next_high, "y", -1)
    with jax.named_scope("experts"):
        near_part = ffn(jnp.concatenate([prev_low, prev_high, next_low, next_high], axis=0))
        far_part = ffn(jnp.concatenate([far_low, far_high], axis=0)).astype(BF16)
        own_part = ffn(after(jnp.concatenate([low, high], axis=0), far_part))
    prev_part, next_part = near_part[: 2 * half], near_part[2 * half :]
    with jax.named_scope("partials_y"):
        early_next = shifted(next_part[half:].astype(BF16), "y", 1)
        early_prev = shifted(prev_part[:half].astype(BF16), "y", -1)
        relay_next = shifted(far_part[:half], "y", 1)
        relay_prev = shifted(far_part[half:], "y", -1)
        late_next = shifted((next_part[:half] + relay_next.astype(F32)).astype(BF16), "y", 1)
        late_prev = shifted((prev_part[half:] + relay_prev.astype(F32)).astype(BF16), "y", -1)
        summed_low = own_part[:half] + late_next.astype(F32) + early_prev.astype(F32)
        summed_high = own_part[half:] + early_next.astype(F32) + late_prev.astype(F32)
        summed_low, summed_high = summed_low.astype(BF16), summed_high.astype(BF16)

    with jax.named_scope("dense_tokens"):
        half_tokens = tok_rows // 2
        by_line = (
            tokens.reshape(tok_rows, 4, 4, step).transpose(2, 0, 1, 3).reshape(4, tok_rows, slab)
        )
        own_half = lax.dynamic_slice_in_dim(by_line, core * half_tokens, half_tokens, axis=1)
        half_in = exchanged(after(own_half, lines[1]), "z")
        other_half = shifted(half_in, "core", 1)
        first = jnp.where(core == 0, half_in, other_half)
        second = jnp.where(core == 0, other_half, half_in)
        line_tokens = jnp.concatenate([first, second], axis=1).reshape(4 * tok_rows, slab)
    slabs = slabs.reshape(4, 3, step, hidden)
    gate_slab, up_slab, down_slab = (slabs[:, i].reshape(slab, hidden) for i in range(3))
    with jax.named_scope("dense_hidden"):
        pre = jnp.concatenate([dot(line_tokens, gate_slab), dot(line_tokens, up_slab)], axis=1)
        pre = pre.astype(BF16).reshape(4, tok_rows, 2 * hidden)
        pre = exchanged(pre, "z")
        pre = jnp.sum(pre.astype(F32), axis=0)
        act = swiglu(pre[:, :hidden], pre[:, hidden:])
        line_act = exchanged(jnp.broadcast_to(act[None], (4,) + act.shape), "z")
        line_act = line_act.reshape(4 * tok_rows, hidden)
    with jax.named_scope("dense_out"):
        contract = (((1,), (1,)), ((), ()))
        dense_out = lax.dot_general(line_act, down_slab, contract, preferred_element_type=F32)
        by_block = (
            dense_out.astype(BF16)
            .reshape(4, 2, half_tokens, 4, step)
            .transpose(3, 1, 0, 2, 4)
            .reshape(n_expert, 4 * half_tokens, step)
        )
        block_sum = jnp.sum(exchanged(by_block, EXPERT_AXES).astype(F32), axis=0).astype(BF16)
        blocks = exchanged(block_sum.reshape(4, half_tokens, step), "z")
        kept = lax.dynamic_slice_in_dim(blocks, 2 * core, 2, axis=0)
        given = lax.dynamic_slice_in_dim(blocks, 2 - 2 * core, 2, axis=0)
        taken = shifted(given, "core", 1)
        first = jnp.where(core == 0, kept, taken)
        second = jnp.where(core == 0, taken, kept)
        dense_total = jnp.concatenate([first, second], axis=1).transpose(1, 0, 2)
    base = residual[0].astype(F32) + dense_total.reshape(tok_rows, piece).astype(F32)

    with jax.named_scope("partials_z"):
        total = summed_low[:capacity].astype(F32)
        for k, (part, by) in enumerate(
            ((summed_low[capacity:], -1), (summed_high[:capacity], -3), (summed_high[capacity:], -2))
        ):
            total = total + shifted(part, "z", by).astype(F32)
        expert_out = total.astype(BF16)
    with jax.named_scope("combine"):
        by_feature = expert_out.reshape(capacity, n_expert, piece).transpose(1, 0, 2)
        returned = exchanged(by_feature, EXPERT_AXES).reshape(n_expert * capacity, piece)
        target = picks * capacity + slot
        columns = jnp.arange(n_expert * capacity, dtype=jnp.int32)
        chosen = jnp.where(columns[None, None, :] == target[:, :, None], weights[:, :, None], 0.0)
        combine = jnp.sum(chosen, axis=1)
        coarse = lax.reduce_precision(combine, 8, 7)
        fine = lax.reduce_precision(combine - coarse, 8, 7)
        spread = dot(coarse.astype(BF16), returned) + dot(fine.astype(BF16), returned)
        mixed = (base + spread).astype(BF16)
    with jax.named_scope("next_section"):
        return shifted(mixed, "section", 1)[None]


def solution(mesh):
    fine_mesh = Mesh(mesh.devices.reshape(GRID), AXES)
    data = ("y", "z")
    placed = (
        P("section", data, None),
        P("section", data, EXPERT_AXES),
        P("section", data, None),
        P("section", data, None),
        P("section", data, EXPERT_AXES),
        P("section", data, EXPERT_AXES),
        P("section", data, EXPERT_AXES),
        P("section", EXPERT_AXES, None, data),
        P("section", EXPERT_AXES, None, data),
        P("section", EXPERT_AXES, data, None),
    )
    return jax.shard_map(
        body,
        mesh=fine_mesh,
        in_specs=placed,
        out_specs=P("section", data, EXPERT_AXES),
        check_vma=False,
    )
```

```python
import jax
import jax.numpy as jnp
from jax import lax
from jax.sharding import Mesh, PartitionSpec as P

AXES = ("section", "y", "z", "x", "core")
GRID = (4, 4, 4, 4, 2)
EXPERT_AXES = ("x", "core")
BF16, F32 = jnp.bfloat16, jnp.float32


def shifted(x, axis, by):
    peers = lax.axis_size(axis)
    return lax.ppermute(x, axis, [(i, (i + by) % peers) for i in range(peers)])


def exchanged(x, axes):
    return lax.all_to_all(x, axes, split_axis=0, concat_axis=0, tiled=True)


def after(x, *others):
    return lax.optimization_barrier((x,) + others)[0]


def swiglu(first, second):
    return (jax.nn.silu(first) * second).astype(BF16)


def dot(a, b):
    return jnp.dot(a, b, preferred_element_type=F32)


def slots_of(picks, n_expert):
    labels = jnp.arange(n_expert, dtype=jnp.int32)
    named = (picks[:, :, None] == labels[None, None, :]).astype(jnp.int32)
    per_token = jnp.sum(named, axis=1, dtype=jnp.int32)
    earlier = jnp.cumsum(per_token, axis=0, dtype=jnp.int32) - per_token
    return jnp.sum(named * earlier[:, None, :], axis=2, dtype=jnp.int32)


def body(
    normed,
    residual,
    expert_index,
    pick_weight,
    dense_gate,
    dense_up,
    dense_down,
    expert_gate,
    expert_up,
    expert_down,
):
    tokens = normed[0]
    picks = expert_index[0]
    weights = pick_weight[0]
    tok_rows, width = tokens.shape
    n_expert = 8
    capacity = min(tok_rows, 9 * tok_rows // (4 * n_expert))
    core = lax.axis_index("core")
    mine = lax.axis_index("x") * 2 + core
    hidden = dense_gate.shape[2]
    slab = width // 4
    step = dense_gate.shape[1]
    piece = width // n_expert

    with jax.named_scope("dense_weights"):
        stacked = jnp.concatenate([dense_gate[0], dense_up[0], dense_down[0]], axis=1)
        slabs = lax.all_gather(stacked, "y", axis=0, tiled=True)
        picks = after(picks, stacked)

    with jax.named_scope("dispatch"):
        slot = slots_of(picks, n_expert)
        is_mine = picks == mine
        positions = jnp.arange(capacity, dtype=jnp.int32)
        select = jnp.any(
            (positions[:, None, None] == slot[None, :, :]) & is_mine[None, :, :], axis=2
        ).astype(BF16)
        routed = dot(select, tokens).astype(BF16)

    with jax.named_scope("rows_z"):
        lines = [routed] + [shifted(routed, "z", by) for by in (1, 3, 2)]
        low = jnp.concatenate([lines[0], lines[1]], axis=0)
        high = jnp.concatenate([lines[2], lines[3]], axis=0)

    with jax.named_scope("dense_tokens"):
        half_tokens = tok_rows // 2
        by_line = (
            tokens.reshape(tok_rows, 4, 4, step).transpose(2, 0, 1, 3).reshape(4, tok_rows, slab)
        )
        own_half = lax.dynamic_slice_in_dim(by_line, core * half_tokens, half_tokens, axis=1)
        half_in = exchanged(after(own_half, lines[1]), "z")
        other_half = shifted(half_in, "core", 1)
        first = jnp.where(core == 0, half_in, other_half)
        second = jnp.where(core == 0, other_half, half_in)
        line_tokens = jnp.concatenate([first, second], axis=1).reshape(4 * tok_rows, slab)
        pre = dot(line_tokens, slabs[:, : 2 * hidden]).astype(BF16)
        pre = pre.reshape(4, tok_rows, 2 * hidden)

    gate_up = jnp.concatenate([expert_gate[0, 0], expert_up[0, 0]], axis=1)
    down = expert_down[0, 0]
    inner = down.shape[0]

    def activate(rows):
        both = dot(rows, gate_up)
        return swiglu(both[:, :inner], both[:, inner:])

    half = 2 * capacity
    with jax.named_scope("rows_y"):
        prev_low, next_low = shifted(low, "y", 1), shifted(low, "y", -1)
        far_low = shifted(prev_low, "y", 1)
        next_high, prev_high = shifted(high, "y", -1), shifted(high, "y", 1)
        far_high = shifted(next_high, "y", -1)
    with jax.named_scope("experts"):
        far_act = activate(after(jnp.concatenate([far_low, far_high], axis=0), pre))
        relay_next = dot(far_act[:half], down).astype(BF16)
        relay_prev = dot(far_act[half:], down).astype(BF16)
        near = jnp.concatenate([next_high, prev_low, next_low, prev_high], axis=0)
        near_act = activate(after(near, relay_next, relay_prev))
        early_next = dot(near_act[:half], down).astype(BF16)
        early_prev = dot(near_act[half : 2 * half], down).astype(BF16)
        own_low, own_high = after((low, high), early_next, early_prev)
        own_low, own_high = activate(own_low), activate(own_high)
    with jax.named_scope("partials_y"):
        relay_next, relay_prev = shifted(relay_next, "y", 1), shifted(relay_prev, "y", -1)
        early_next, early_prev = shifted(early_next, "y", 1), shifted(early_prev, "y", -1)
        late_next = dot(near_act[2 * half : 3 * half], down) + relay_next.astype(F32)
        late_prev = dot(near_act[3 * half :], down) + relay_prev.astype(F32)
        late_next = shifted(late_next.astype(BF16), "y", 1)
        late_prev = shifted(late_prev.astype(BF16), "y", -1)
        total = [
            dot(act[rows], down) + one[rows].astype(F32) + two[rows].astype(F32)
            for act, one, two in ((own_low, late_next, early_prev), (own_high, early_next, late_prev))
            for rows in (slice(0, capacity), slice(capacity, half))
        ]

    with jax.named_scope("dense_hidden"):
        pre = exchanged(pre, "z")
        pre = jnp.sum(pre.astype(F32), axis=0)
        act = swiglu(pre[:, :hidden], pre[:, hidden:])
        line_act = exchanged(jnp.broadcast_to(act[None], (4,) + act.shape), "z")
        line_act = line_act.reshape(4 * tok_rows, hidden)
    with jax.named_scope("dense_out"):
        contract = (((1,), (1,)), ((), ()))
        dense_out = lax.dot_general(
            line_act, slabs[:, 2 * hidden :], contract, preferred_element_type=F32
        )
        by_block = (
            dense_out.astype(BF16)
            .reshape(4, 2, half_tokens, 4, step)
            .transpose(3, 1, 0, 2, 4)
            .reshape(n_expert, 4 * half_tokens, step)
        )
        block_sum = jnp.sum(exchanged(by_block, EXPERT_AXES).astype(F32), axis=0).astype(BF16)
        blocks = exchanged(block_sum.reshape(4, half_tokens, step), "z")
        kept = lax.dynamic_slice_in_dim(blocks, 2 * core, 2, axis=0)
        given = lax.dynamic_slice_in_dim(blocks, 2 - 2 * core, 2, axis=0)
        taken = shifted(given, "core", 1)
        first = jnp.where(core == 0, kept, taken)
        second = jnp.where(core == 0, taken, kept)
        dense_total = jnp.concatenate([first, second], axis=1).transpose(1, 0, 2)
    base = residual[0].astype(F32) + dense_total.reshape(tok_rows, piece).astype(F32)

    with jax.named_scope("partials_z"):
        expert_out = total[0]
        for part, by in zip(total[1:], (-1, -3, -2)):
            expert_out = expert_out + shifted(part.astype(BF16), "z", by).astype(F32)
        expert_out = expert_out.astype(BF16)
    with jax.named_scope("combine"):
        by_feature = expert_out.reshape(capacity, n_expert, piece).transpose(1, 0, 2)
        returned = exchanged(by_feature, EXPERT_AXES).reshape(n_expert * capacity, piece)
        target = picks * capacity + slot
        columns = jnp.arange(n_expert * capacity, dtype=jnp.int32)
        chosen = jnp.where(columns[None, None, :] == target[:, :, None], weights[:, :, None], 0.0)
        combine = jnp.sum(chosen, axis=1)
        coarse = lax.reduce_precision(combine, 8, 7)
        fine = lax.reduce_precision(combine - coarse, 8, 7)
        spread = dot(coarse.astype(BF16), returned) + dot(fine.astype(BF16), returned)
        mixed = (base + spread).astype(BF16)
    with jax.named_scope("next_section"):
        return shifted(mixed, "section", 1)[None]


def solution(mesh):
    fine_mesh = Mesh(mesh.devices.reshape(GRID), AXES)
    data = ("y", "z")
    placed = (
        P("section", data, None),
        P("section", data, EXPERT_AXES),
        P("section", data, None),
        P("section", data, None),
        P("section", data, EXPERT_AXES),
        P("section", data, EXPERT_AXES),
        P("section", data, EXPERT_AXES),
        P("section", EXPERT_AXES, None, data),
        P("section", EXPERT_AXES, None, data),
        P("section", EXPERT_AXES, data, None),
    )
    return jax.shard_map(
        body,
        mesh=fine_mesh,
        in_specs=placed,
        out_specs=P("section", data, EXPERT_AXES),
        check_vma=False,
    )
```

```python
import jax
import jax.numpy as jnp
from jax import lax
from jax.sharding import Mesh, PartitionSpec as P

AXES = ("section", "y", "z", "x", "core")
GRID = (4, 4, 4, 4, 2)
EXPERT_AXES = ("x", "core")
BF16, F32 = jnp.bfloat16, jnp.float32


def shifted(x, axis, by):
    peers = lax.axis_size(axis)
    return lax.ppermute(x, axis, [(i, (i + by) % peers) for i in range(peers)])


def exchanged(x, axes):
    return lax.all_to_all(x, axes, split_axis=0, concat_axis=0, tiled=True)


def after(x, *others):
    return lax.optimization_barrier((x,) + others)[0]


def swiglu(first, second):
    return (jax.nn.silu(first) * second).astype(BF16)


def dot(a, b):
    return jnp.dot(a, b, preferred_element_type=F32)


def slots_of(picks, n_expert):
    labels = jnp.arange(n_expert, dtype=jnp.int32)
    named = (picks[:, :, None] == labels[None, None, :]).astype(jnp.int32)
    per_token = jnp.sum(named, axis=1, dtype=jnp.int32)
    earlier = jnp.cumsum(per_token, axis=0, dtype=jnp.int32) - per_token
    return jnp.sum(named * earlier[:, None, :], axis=2, dtype=jnp.int32)


def body(
    normed,
    residual,
    expert_index,
    pick_weight,
    dense_gate,
    dense_up,
    dense_down,
    expert_gate,
    expert_up,
    expert_down,
):
    tokens = normed[0]
    picks = expert_index[0]
    weights = pick_weight[0]
    tok_rows, width = tokens.shape
    n_expert = 8
    capacity = min(tok_rows, 9 * tok_rows // (4 * n_expert))
    core = lax.axis_index("core")
    mine = lax.axis_index("x") * 2 + core
    hidden = dense_gate.shape[2]
    slab = width // 4
    step = dense_gate.shape[1]
    piece = width // n_expert

    with jax.named_scope("dense_weights"):
        stacked = jnp.concatenate([dense_gate[0], dense_up[0], dense_down[0]], axis=1)
        slabs = lax.all_gather(stacked, "y", axis=0, tiled=True)
        picks = after(picks, stacked)

    with jax.named_scope("dispatch"):
        slot = slots_of(picks, n_expert)
        is_mine = picks == mine
        positions = jnp.arange(capacity, dtype=jnp.int32)
        select = jnp.any(
            (positions[:, None, None] == slot[None, :, :]) & is_mine[None, :, :], axis=2
        ).astype(BF16)
        routed = dot(select, tokens).astype(BF16)

    with jax.named_scope("rows_z"):
        lines = [routed] + [shifted(routed, "z", by) for by in (1, 3, 2)]
        low = jnp.concatenate([lines[0], lines[1]], axis=0)
        high = jnp.concatenate([lines[2], lines[3]], axis=0)

    with jax.named_scope("dense_tokens"):
        half_tokens = tok_rows // 2
        by_line = (
            tokens.reshape(tok_rows, 4, 4, step).transpose(2, 0, 1, 3).reshape(4, tok_rows, slab)
        )
        own_half = lax.dynamic_slice_in_dim(by_line, core * half_tokens, half_tokens, axis=1)
        half_in = exchanged(after(own_half, lines[1], lines[2]), "z")
        other_half = shifted(half_in, "core", 1)
        first = jnp.where(core == 0, half_in, other_half)
        second = jnp.where(core == 0, other_half, half_in)
        line_tokens = jnp.concatenate([first, second], axis=1).reshape(4 * tok_rows, slab)
        pre = dot(line_tokens, slabs[:, : 2 * hidden]).astype(BF16)
        pre = pre.reshape(4, tok_rows, 2 * hidden)

    gate_up = jnp.concatenate([expert_gate[0, 0], expert_up[0, 0]], axis=1)
    down = expert_down[0, 0]
    inner = down.shape[0]

    def activate(rows):
        both = dot(rows, gate_up)
        return swiglu(both[:, :inner], both[:, inner:])

    half = 2 * capacity
    with jax.named_scope("rows_y"):
        prev_low, next_low = shifted(low, "y", 1), shifted(low, "y", -1)
        far_low = shifted(prev_low, "y", 1)
        next_high, prev_high = shifted(high, "y", -1), shifted(high, "y", 1)
        far_high = shifted(next_high, "y", -1)
    with jax.named_scope("experts"):
        next_high, prev_low = after((next_high, prev_low), pre)
        early_next = dot(activate(next_high), down).astype(BF16)
        early_prev = dot(activate(prev_low), down).astype(BF16)
        next_act, prev_act = activate(next_low), activate(prev_high)
        far_low, far_high = after((far_low, far_high), early_next, early_prev)
        relay_next = dot(activate(far_low), down).astype(BF16)
        relay_prev = dot(activate(far_high), down).astype(BF16)
        own_low, own_high = after((low, high), relay_next, relay_prev)
        own_low, own_high = activate(own_low), activate(own_high)
    with jax.named_scope("partials_y"):
        relay_next, relay_prev = shifted(relay_next, "y", 1), shifted(relay_prev, "y", -1)
        early_next, early_prev = shifted(early_next, "y", 1), shifted(early_prev, "y", -1)
        late_next = dot(next_act, down) + relay_next.astype(F32)
        late_prev = dot(prev_act, down) + relay_prev.astype(F32)
        late_next = shifted(late_next.astype(BF16), "y", 1)
        late_prev = shifted(late_prev.astype(BF16), "y", -1)
        total = [
            dot(act[rows], down) + one[rows].astype(F32) + two[rows].astype(F32)
            for act, one, two in ((own_low, late_next, early_prev), (own_high, early_next, late_prev))
            for rows in (slice(0, capacity), slice(capacity, half))
        ]

    with jax.named_scope("dense_hidden"):
        pre = exchanged(pre, "z")
        pre = jnp.sum(pre.astype(F32), axis=0)
        act = swiglu(pre[:, :hidden], pre[:, hidden:])
        line_act = exchanged(jnp.broadcast_to(act[None], (4,) + act.shape), "z")
        line_act = line_act.reshape(4 * tok_rows, hidden)
    with jax.named_scope("dense_out"):
        contract = (((1,), (1,)), ((), ()))
        dense_out = lax.dot_general(
            line_act, slabs[:, 2 * hidden :], contract, preferred_element_type=F32
        )
        by_block = (
            dense_out.astype(BF16)
            .reshape(4, 2, half_tokens, 4, step)
            .transpose(3, 1, 0, 2, 4)
            .reshape(n_expert, 4 * half_tokens, step)
        )
        block_sum = jnp.sum(exchanged(by_block, EXPERT_AXES).astype(F32), axis=0).astype(BF16)
        blocks = exchanged(block_sum.reshape(4, half_tokens, step), "z")
        kept = lax.dynamic_slice_in_dim(blocks, 2 * core, 2, axis=0)
        given = lax.dynamic_slice_in_dim(blocks, 2 - 2 * core, 2, axis=0)
        taken = shifted(given, "core", 1)
        first = jnp.where(core == 0, kept, taken)
        second = jnp.where(core == 0, taken, kept)
        dense_total = jnp.concatenate([first, second], axis=1).transpose(1, 0, 2)
    base = residual[0].astype(F32) + dense_total.reshape(tok_rows, piece).astype(F32)

    with jax.named_scope("partials_z"):
        expert_out = total[0]
        for part, by in zip(total[1:], (-1, -3, -2)):
            expert_out = expert_out + shifted(part.astype(BF16), "z", by).astype(F32)
        expert_out = expert_out.astype(BF16)
    with jax.named_scope("combine"):
        by_feature = expert_out.reshape(capacity, n_expert, piece).transpose(1, 0, 2)
        returned = exchanged(by_feature, EXPERT_AXES).reshape(n_expert * capacity, piece)
        target = picks * capacity + slot
        columns = jnp.arange(n_expert * capacity, dtype=jnp.int32)
        chosen = jnp.where(columns[None, None, :] == target[:, :, None], weights[:, :, None], 0.0)
        combine = jnp.sum(chosen, axis=1)
        coarse = lax.reduce_precision(combine, 8, 7)
        fine = lax.reduce_precision(combine - coarse, 8, 7)
        spread = dot(coarse.astype(BF16), returned) + dot(fine.astype(BF16), returned)
        mixed = (base + spread).astype(BF16)
    with jax.named_scope("next_section"):
        return shifted(mixed, "section", 1)[None]


def solution(mesh):
    fine_mesh = Mesh(mesh.devices.reshape(GRID), AXES)
    data = ("y", "z")
    placed = (
        P("section", data, None),
        P("section", data, EXPERT_AXES),
        P("section", data, None),
        P("section", data, None),
        P("section", data, EXPERT_AXES),
        P("section", data, EXPERT_AXES),
        P("section", data, EXPERT_AXES),
        P("section", EXPERT_AXES, None, data),
        P("section", EXPERT_AXES, None, data),
        P("section", EXPERT_AXES, data, None),
    )
    return jax.shard_map(
        body,
        mesh=fine_mesh,
        in_specs=placed,
        out_specs=P("section", data, EXPERT_AXES),
        check_vma=False,
    )
```

```python
import jax
import jax.numpy as jnp
from jax import lax
from jax.sharding import Mesh, PartitionSpec as P

AXES = ("section", "y", "z", "x", "core")
GRID = (4, 4, 4, 4, 2)
EXPERT_AXES = ("x", "core")
BF16, F32 = jnp.bfloat16, jnp.float32


def shifted(x, axis, by):
    peers = lax.axis_size(axis)
    return lax.ppermute(x, axis, [(i, (i + by) % peers) for i in range(peers)])


def exchanged(x, axes):
    return lax.all_to_all(x, axes, split_axis=0, concat_axis=0, tiled=True)


def after(x, *others):
    return lax.optimization_barrier((x,) + others)[0]


def swiglu(first, second):
    return (jax.nn.silu(first) * second).astype(BF16)


def dot(a, b):
    return jnp.dot(a, b, preferred_element_type=F32)


def slots_of(picks, n_expert):
    labels = jnp.arange(n_expert, dtype=jnp.int32)
    named = (picks[:, :, None] == labels[None, None, :]).astype(jnp.int32)
    per_token = jnp.sum(named, axis=1, dtype=jnp.int32)
    earlier = jnp.cumsum(per_token, axis=0, dtype=jnp.int32) - per_token
    return jnp.sum(named * earlier[:, None, :], axis=2, dtype=jnp.int32)


def body(
    normed,
    residual,
    expert_index,
    pick_weight,
    dense_gate,
    dense_up,
    dense_down,
    expert_gate,
    expert_up,
    expert_down,
):
    tokens = normed[0]
    picks = expert_index[0]
    weights = pick_weight[0]
    tok_rows, width = tokens.shape
    n_expert = 8
    capacity = min(tok_rows, 9 * tok_rows // (4 * n_expert))
    core = lax.axis_index("core")
    mine = lax.axis_index("x") * 2 + core
    hidden = dense_gate.shape[2]
    slab = width // 4
    step = dense_gate.shape[1]
    piece = width // n_expert

    with jax.named_scope("dispatch"):
        slot = slots_of(picks, n_expert)
        is_mine = picks == mine
        positions = jnp.arange(capacity, dtype=jnp.int32)
        select = jnp.any(
            (positions[:, None, None] == slot[None, :, :]) & is_mine[None, :, :], axis=2
        ).astype(BF16)
        routed = dot(select, tokens).astype(BF16)

    with jax.named_scope("dense_weights"):
        stacked = jnp.concatenate([dense_gate[0], dense_up[0], dense_down[0]], axis=1)
        stacked = jnp.broadcast_to(after(stacked, routed)[None], (4,) + stacked.shape)
        slabs = exchanged(stacked, "y").reshape(slab, 3 * hidden)

    with jax.named_scope("combine"):
        target = picks * capacity + slot
        columns = jnp.arange(n_expert * capacity, dtype=jnp.int32)
        chosen = jnp.where(columns[None, None, :] == target[:, :, None], weights[:, :, None], 0.0)
        combine = jnp.sum(chosen, axis=1)
        coarse = lax.reduce_precision(combine, 8, 7)
        fine = lax.reduce_precision(combine - coarse, 8, 7)
        coarse, fine = coarse.astype(BF16), fine.astype(BF16)

    gate_up = jnp.concatenate([expert_gate[0, 0], expert_up[0, 0]], axis=1)
    down = expert_down[0, 0]
    inner = down.shape[0]

    with jax.named_scope("rows_z"):
        lines = [routed] + [shifted(routed, "z", by) for by in (1, 3, 2)]
        low = jnp.concatenate([lines[0], lines[1]], axis=0)
        high = jnp.concatenate([lines[2], lines[3]], axis=0)
        gate_up, coarse, fine = after((gate_up, coarse, fine), routed)
        low = after(low, gate_up, coarse, fine)

    half = 2 * capacity
    with jax.named_scope("rows_y"):
        prev_low, next_low = shifted(low, "y", 1), shifted(low, "y", -1)
        far_low = shifted(prev_low, "y", 1)
        next_high, prev_high = shifted(high, "y", -1), shifted(high, "y", 1)
        far_high = shifted(next_high, "y", -1)

    with jax.named_scope("dense_tokens"):
        half_tokens = tok_rows // 2
        by_line = (
            tokens.reshape(tok_rows, 4, 4, step).transpose(2, 0, 1, 3).reshape(4, tok_rows, slab)
        )
        own_half = lax.dynamic_slice_in_dim(by_line, core * half_tokens, half_tokens, axis=1)
        half_in = exchanged(after(own_half, slabs, low, high), "z")
        half_in = after(half_in, prev_low, next_low, prev_high, next_high)
        other_half = shifted(half_in, "core", 1)
        first = jnp.where(core == 0, half_in, other_half)
        second = jnp.where(core == 0, other_half, half_in)
        line_tokens = jnp.concatenate([first, second], axis=1).reshape(4 * tok_rows, slab)
        pre = dot(line_tokens, slabs[:, : 2 * hidden]).astype(BF16)
        pre = pre.reshape(4, tok_rows, 2 * hidden)

    def activate(rows, *first):
        both = dot(rows, after(gate_up, *first))
        return swiglu(both[:, :inner], both[:, inner:])

    with jax.named_scope("experts"):
        early_next = dot(activate(next_high, pre), down).astype(BF16)
        early_prev = dot(activate(prev_low, pre), down).astype(BF16)
        next_act, prev_act = activate(next_low, pre), activate(prev_high, pre)
        done = (early_next, early_prev, next_act, prev_act)
        relay_next = dot(activate(far_low, *done), down).astype(BF16)
        relay_prev = dot(activate(far_high, *done), down).astype(BF16)

    with jax.named_scope("dense_hidden"):
        pre = exchanged(pre, "z")
        pre = jnp.sum(pre.astype(F32), axis=0)
        act = swiglu(pre[:, :hidden], pre[:, hidden:])
        line_act = jnp.broadcast_to(act[None], (4,) + act.shape)
    with jax.named_scope("dense_out"):
        every_act = exchanged(line_act, "z").reshape(4 * tok_rows, hidden)
        contract = (((1,), (1,)), ((), ()))
        dense_out = lax.dot_general(
            every_act, slabs[:, 2 * hidden :], contract, preferred_element_type=F32
        )
        by_block = (
            dense_out.astype(BF16)
            .reshape(4, 2, half_tokens, 4, step)
            .transpose(3, 1, 0, 2, 4)
            .reshape(n_expert, 4 * half_tokens, step)
        )

    with jax.named_scope("partials_y"):
        relay_next, relay_prev = shifted(relay_next, "y", 1), shifted(relay_prev, "y", -1)
        relay_next, relay_prev = after((relay_next, relay_prev), line_act)
        early_next, early_prev = shifted(early_next, "y", 1), shifted(early_prev, "y", -1)
        late_next = dot(next_act, down) + relay_next.astype(F32)
        late_prev = dot(prev_act, down) + relay_prev.astype(F32)
        late_next, late_prev = late_next.astype(BF16), late_prev.astype(BF16)
        done = (late_next, late_prev)
        own_low, own_high = activate(low, *done), activate(high, *done)
        late_next, late_prev = shifted(late_next, "y", 1), shifted(late_prev, "y", -1)
        total = [
            dot(act[rows], down) + one[rows].astype(F32) + two[rows].astype(F32)
            for act, one, two in ((own_low, late_next, early_prev), (own_high, early_next, late_prev))
            for rows in (slice(0, capacity), slice(capacity, half))
        ]

    with jax.named_scope("partials_z"):
        recv = [shifted(part.astype(BF16), "z", by) for part, by in zip(total[1:], (-1, -3, -2))]
        expert_out = total[0] + sum(part.astype(F32) for part in recv)
        expert_out = expert_out.astype(BF16)

    with jax.named_scope("dense_out"):
        block_sum = jnp.sum(exchanged(by_block, EXPERT_AXES).astype(F32), axis=0).astype(BF16)
        block_sum = after(block_sum, recv[0])
        blocks = exchanged(block_sum.reshape(4, half_tokens, step), "z")
        kept = lax.dynamic_slice_in_dim(blocks, 2 * core, 2, axis=0)
        given = lax.dynamic_slice_in_dim(blocks, 2 - 2 * core, 2, axis=0)
        taken = shifted(given, "core", 1)
        first = jnp.where(core == 0, kept, taken)
        second = jnp.where(core == 0, taken, kept)
        dense_total = jnp.concatenate([first, second], axis=1).transpose(1, 0, 2)
    base = residual[0].astype(F32) + dense_total.reshape(tok_rows, piece).astype(F32)

    with jax.named_scope("combine"):
        by_feature = expert_out.reshape(capacity, n_expert, piece).transpose(1, 0, 2)
        by_feature = after(by_feature, blocks)
        returned = exchanged(by_feature, EXPERT_AXES).reshape(n_expert * capacity, piece)
        spread = dot(coarse, returned) + dot(fine, returned)
        mixed = (base + spread).astype(BF16)
    with jax.named_scope("next_section"):
        return shifted(mixed, "section", 1)[None]


def solution(mesh):
    fine_mesh = Mesh(mesh.devices.reshape(GRID), AXES)
    data = ("y", "z")
    placed = (
        P("section", data, None),
        P("section", data, EXPERT_AXES),
        P("section", data, None),
        P("section", data, None),
        P("section", data, EXPERT_AXES),
        P("section", data, EXPERT_AXES),
        P("section", data, EXPERT_AXES),
        P("section", EXPERT_AXES, None, data),
        P("section", EXPERT_AXES, None, data),
        P("section", EXPERT_AXES, data, None),
    )
    return jax.shard_map(
        body,
        mesh=fine_mesh,
        in_specs=placed,
        out_specs=P("section", data, EXPERT_AXES),
        check_vma=False,
    )
```

```python
import functools

import jax
import jax.numpy as jnp
from jax import lax
from jax.experimental import pallas as pl
from jax.experimental.pallas import tpu as pltpu
from jax.sharding import Mesh, PartitionSpec as P

AXES = ("section", "y", "z", "x", "core")
GRID = (4, 4, 4, 4, 2)
EXPERT_AXES = ("x", "core")
BF16, F32 = jnp.bfloat16, jnp.float32


def shifted(x, axis, by):
    peers = lax.axis_size(axis)
    return lax.ppermute(x, axis, [(i, (i + by) % peers) for i in range(peers)])


def exchanged(x, axes):
    return lax.all_to_all(x, axes, split_axis=0, concat_axis=0, tiled=True)


def repeated(x, times):
    return jnp.broadcast_to(x[None], (times,) + x.shape)


def after(x, *others):
    return lax.optimization_barrier((x,) + others)[0]


def swiglu(first, second):
    return (jax.nn.silu(first) * second).astype(BF16)


def dot(a, b):
    return jnp.dot(a, b, preferred_element_type=F32)


def slots_of(picks, n_expert):
    labels = jnp.arange(n_expert, dtype=jnp.int32)
    named = (picks[:, :, None] == labels[None, None, :]).astype(jnp.int32)
    per_token = jnp.sum(named, axis=1, dtype=jnp.int32)
    earlier = jnp.cumsum(per_token, axis=0, dtype=jnp.int32) - per_token
    return jnp.sum(named * earlier[:, None, :], axis=2, dtype=jnp.int32)


def local_call(kernel, out_shape, **kwargs):
    return pl.pallas_call(
        kernel,
        out_shape=out_shape,
        compiler_params=pltpu.CompilerParams(vmem_limit_bytes=52 * 1024 * 1024),
        cost_estimate=pl.CostEstimate(
            flops=2 * 1024**3, bytes_accessed=4 * 1024**2, transcendentals=0
        ),
        **kwargs,
    )


def expert_rows(parts, gate_up, down):
    inner = down.shape[0]
    rows = jnp.concatenate([part[...].astype(F32) for part in parts], axis=0).astype(BF16)
    both = dot(rows, gate_up[...])
    start = both.shape[1] // 2
    first, second = both[:, :inner], both[:, start : start + inner]
    return dot((first / (1.0 + jnp.exp(-first)) * second).astype(BF16), down[...])


def rows_kernel(gate_up, down, *refs):
    parts, outs = refs[: len(refs) // 2], refs[len(refs) // 2 :]
    result = expert_rows(parts, gate_up, down)
    size = parts[0].shape[0]
    for k, out in enumerate(outs):
        out[...] = result[k * size : (k + 1) * size].astype(out.dtype)


def rows_and_dense_kernel(columns, place, own, other, *refs):
    weights, pre = refs[:4], refs[-1]
    joined = jnp.concatenate([part[:, :columns] for part in weights], axis=0)
    for z in range(4):
        shares = [side[k, z] for side in (own, other) for k in range(4)]
        size = shares[0].shape[0]
        result = dot(jnp.concatenate(shares, axis=0), joined).astype(BF16)
        for i in range(len(shares)):
            start = pl.multiple_of(place[i] * size, size)
            pre[z, pl.ds(start, size)] = result[i * size : (i + 1) * size]
    rows_kernel(*refs[4:-1])


def late_kernel(part, relay, out):
    out[...] = (part[...] + relay[...].astype(F32)).astype(BF16)


def total_kernel(capacity, place, low, high, *refs):
    sums, outs, whole = refs[:4], refs[4:8], refs[8]
    half = 2 * capacity
    whole[:half] = low[...] + sums[0][...].astype(F32) + sums[1][...].astype(F32)
    whole[half:] = high[...] + sums[2][...].astype(F32) + sums[3][...].astype(F32)
    for k, out in enumerate(outs):
        for j in range(4):

            @pl.when(place[k] == j)
            def _(out=out, j=j):
                out[...] = whole[j * capacity : (j + 1) * capacity].astype(out.dtype)


def in_line_order(parts, axis):
    order = (lax.axis_index(axis) - jnp.arange(4, dtype=jnp.int32)) % 4
    return jnp.stack(parts).at[order].get(mode="promise_in_bounds")


def dense_out_kernel(columns, place, act, *refs):
    weights, out = refs[:4], refs[4]
    contract = (((1,), (1,)), ((), ()))
    for k in range(4):
        part = lax.dot_general(
            act[...], weights[k][:, columns:], contract, preferred_element_type=F32
        ).astype(BF16)
        half = part.shape[0] // 8
        for side in range(2):
            pieces = [part[(2 * j + side) * half : (2 * j + side + 1) * half] for j in range(4)]
            out[2 * place[k] + side] = jnp.concatenate(pieces, axis=0)


def body(
    normed,
    residual,
    expert_index,
    pick_weight,
    dense_gate,
    dense_up,
    dense_down,
    expert_gate,
    expert_up,
    expert_down,
):
    tokens = normed[0]
    picks = expert_index[0]
    weights = pick_weight[0]
    tok_rows, width = tokens.shape
    n_expert = 8
    capacity = min(tok_rows, 9 * tok_rows // (4 * n_expert))
    core = lax.axis_index("core")
    mine = lax.axis_index("x") * 2 + core
    hidden = dense_gate.shape[2]
    slab = width // 4
    step = dense_gate.shape[1]
    piece = width // n_expert

    with jax.named_scope("dispatch"):
        slot = slots_of(picks, n_expert)
        is_mine = picks == mine
        positions = jnp.arange(capacity, dtype=jnp.int32)
        select = jnp.any(
            (positions[:, None, None] == slot[None, :, :]) & is_mine[None, :, :], axis=2
        ).astype(BF16)
        routed = dot(select, tokens).astype(BF16)

    with jax.named_scope("dense_weights"):
        stacked = jnp.concatenate([dense_gate[0], dense_up[0], dense_down[0]], axis=1)
        stacked = after(stacked, routed)
        slabs = [stacked] + [shifted(stacked, "y", by) for by in (1, 2, 3)]
        steps_back = jnp.arange(4, dtype=jnp.int32)
        place_y, place_z = ((lax.axis_index(axis) - steps_back) % 4 for axis in ("y", "z"))

    with jax.named_scope("combine"):
        target = picks * capacity + slot
        columns = jnp.arange(n_expert * capacity, dtype=jnp.int32)
        chosen = jnp.where(columns[None, None, :] == target[:, :, None], weights[:, :, None], 0.0)
        combine = jnp.sum(chosen, axis=1)
        coarse = lax.reduce_precision(combine, 8, 7)
        fine = lax.reduce_precision(combine - coarse, 8, 7)
        coarse, fine = coarse.astype(BF16), fine.astype(BF16)

    down = expert_down[0, 0]
    blank = jnp.zeros((width, -down.shape[0] % 256), BF16)
    gate_up = jnp.concatenate([expert_gate[0, 0], blank, expert_up[0, 0], blank], axis=1)

    half = 2 * capacity
    with jax.named_scope("rows_z"):
        share = tok_rows // n_expert
        own_share = lax.dynamic_slice_in_dim(tokens, mine * share, share, axis=0)
        own_share = own_share.reshape(share, 4, 4, step)
        own_share = own_share.at[:, place_y].get(mode="promise_in_bounds").transpose(2, 0, 1, 3)
        sent = [repeated(routed, 4), own_share.reshape(4, share // 4, width)]
        arrived = exchanged(jnp.concatenate(sent, axis=1), "z")
        line_share = arrived[:, capacity:].reshape(4, share, slab)
        coarse, fine, gate_up = after((coarse, fine, gate_up), routed)
        group = after(arrived, coarse, fine, gate_up, *slabs[1:])[:, :capacity]
        low, high = (block.reshape(half, width) for block in (group[:2], group[2:]))

    with jax.named_scope("rows_y"):
        prev_low, next_low = shifted(low, "y", 1), shifted(low, "y", -1)
        far_low = shifted(prev_low, "y", 1)
        next_high, prev_high = shifted(high, "y", -1), shifted(high, "y", 1)
        far_high = shifted(next_high, "y", -1)

    with jax.named_scope("dense_tokens"):
        own_shares = jnp.stack([line_share] + [shifted(line_share, "x", by) for by in (1, 2, 3)])
        other_shares = shifted(own_shares, "core", 1)
        place_x = (lax.axis_index("x") - steps_back) % 4
        place_share = jnp.concatenate([2 * place_x + core, 2 * place_x + 1 - core])

    half_bf16, half_f32 = (jax.ShapeDtypeStruct(low.shape, dtype) for dtype in (BF16, F32))
    in_smem, in_vmem = (pl.BlockSpec(memory_space=space) for space in (pltpu.SMEM, pltpu.VMEM))
    with jax.named_scope("experts"):
        relay_next, relay_prev, early_next, early_prev, next_part, prev_part, pre = local_call(
            functools.partial(rows_and_dense_kernel, 2 * hidden),
            [half_bf16] * 4
            + [half_f32] * 2
            + [jax.ShapeDtypeStruct((4, tok_rows, 2 * hidden), BF16)],
            in_specs=[in_smem] + [in_vmem] * 14,
        )(
            place_share,
            own_shares,
            other_shares,
            *slabs,
            gate_up,
            down,
            *(far_low, far_high, next_high, prev_low, next_low, prev_high),
        )

    with jax.named_scope("dense_hidden"):
        pre = exchanged(pre, "z")
        pre = jnp.sum(pre.astype(F32), axis=0)
        act = swiglu(pre[:, :hidden], pre[:, hidden:])
        line_act = jnp.broadcast_to(act[None], (4,) + act.shape)
    with jax.named_scope("dense_out"):
        half_tokens = tok_rows // 2
        every_act = exchanged(line_act, "z").reshape(4 * tok_rows, hidden)
        by_block = local_call(
            functools.partial(dense_out_kernel, 2 * hidden),
            jax.ShapeDtypeStruct((n_expert, 4 * half_tokens, step), BF16),
            in_specs=[in_smem] + [in_vmem] * 5,
        )(place_y, every_act, *slabs)

    with jax.named_scope("partials_y"):
        relay_next, relay_prev = shifted(relay_next, "y", 1), shifted(relay_prev, "y", -1)
        early_next, early_prev = shifted(early_next, "y", 1), shifted(early_prev, "y", -1)
        late_next = local_call(late_kernel, half_bf16)(next_part, relay_next)
        late_prev = local_call(late_kernel, half_bf16)(prev_part, relay_prev)
        own_low, own_high = local_call(rows_kernel, [half_f32] * 2)(
            after(gate_up, late_next, late_prev), down, low, high
        )
        late_next, late_prev = shifted(late_next, "y", 1), shifted(late_prev, "y", -1)

    with jax.named_scope("partials_z"):
        rows_f32, rows_bf16 = (jax.ShapeDtypeStruct(routed.shape, dtype) for dtype in (F32, BF16))
        kept_rows, *sent = local_call(
            functools.partial(total_kernel, capacity),
            [rows_f32] + [rows_bf16] * 3,
            in_specs=[in_smem] + [in_vmem] * 6,
            scratch_shapes=[pltpu.VMEM((4 * capacity, width), F32)],
        )(place_z, own_low, own_high, late_next, early_prev, early_next, late_prev)
        recv = [shifted(part, "z", by) for part, by in zip(sent, (-1, -2, -3))]
        expert_out = (kept_rows + sum(part.astype(F32) for part in recv)).astype(BF16)

    with jax.named_scope("dense_out"):
        block_sum = jnp.sum(exchanged(by_block, EXPERT_AXES).astype(F32), axis=0).astype(BF16)
        block_sum = block_sum.reshape(4, half_tokens, step)
        blocks = []
        for by in range(4):
            there = (lax.axis_index("z") + by) % 4
            block = lax.dynamic_index_in_dim(block_sum, there, 0, keepdims=False)
            blocks.append(shifted(block, "z", by) if by else block)
        blocks = in_line_order(blocks, "z")
        kept = lax.dynamic_slice_in_dim(blocks, 2 * core, 2, axis=0)
        given = lax.dynamic_slice_in_dim(blocks, 2 - 2 * core, 2, axis=0)
        taken = shifted(given, "core", 1)
        first = jnp.where(core == 0, kept, taken)
        second = jnp.where(core == 0, taken, kept)
        dense_total = jnp.concatenate([first, second], axis=1).transpose(1, 0, 2)
    base = residual[0].astype(F32) + dense_total.reshape(tok_rows, piece).astype(F32)

    with jax.named_scope("combine"):
        by_feature = expert_out.reshape(capacity, n_expert, piece).transpose(1, 0, 2)
        returned = exchanged(by_feature, EXPERT_AXES).reshape(n_expert * capacity, piece)
        spread = dot(coarse, returned) + dot(fine, returned)
        mixed = (base + spread).astype(BF16)
    with jax.named_scope("next_section"):
        return shifted(mixed, "section", 1)[None]


def solution(mesh):
    fine_mesh = Mesh(mesh.devices.reshape(GRID), AXES)
    data = ("y", "z")
    placed = (
        P("section", data, None),
        P("section", data, EXPERT_AXES),
        P("section", data, None),
        P("section", data, None),
        P("section", data, EXPERT_AXES),
        P("section", data, EXPERT_AXES),
        P("section", data, EXPERT_AXES),
        P("section", EXPERT_AXES, None, data),
        P("section", EXPERT_AXES, None, data),
        P("section", EXPERT_AXES, data, None),
    )
    return jax.shard_map(
        body,
        mesh=fine_mesh,
        in_specs=placed,
        out_specs=P("section", data, EXPERT_AXES),
        check_vma=False,
    )
```

```python
import functools

import jax
import jax.numpy as jnp
from jax import lax
from jax.experimental import pallas as pl
from jax.experimental.pallas import tpu as pltpu
from jax.sharding import Mesh, PartitionSpec as P

AXES = ("section", "y", "z", "x", "core")
GRID = (4, 4, 4, 4, 2)
EXPERT_AXES = ("x", "core")
BF16, F32 = jnp.bfloat16, jnp.float32


def shifted(x, axis, by):
    peers = lax.axis_size(axis)
    return lax.ppermute(x, axis, [(i, (i + by) % peers) for i in range(peers)])


def exchanged(x, axes):
    return lax.all_to_all(x, axes, split_axis=0, concat_axis=0, tiled=True)


def repeated(x, times):
    return jnp.broadcast_to(x[None], (times,) + x.shape)


def after(x, *others):
    return lax.optimization_barrier((x,) + others)[0]


def swiglu(first, second):
    return (jax.nn.silu(first) * second).astype(BF16)


def dot(a, b):
    return jnp.dot(a, b, preferred_element_type=F32)


def slots_of(picks, n_expert):
    labels = jnp.arange(n_expert, dtype=jnp.int32)
    named = (picks[:, :, None] == labels[None, None, :]).astype(jnp.int32)
    per_token = jnp.sum(named, axis=1, dtype=jnp.int32)
    earlier = jnp.cumsum(per_token, axis=0, dtype=jnp.int32) - per_token
    return jnp.sum(named * earlier[:, None, :], axis=2, dtype=jnp.int32)


def local_call(kernel, out_shape, **kwargs):
    return pl.pallas_call(
        kernel,
        out_shape=out_shape,
        compiler_params=pltpu.CompilerParams(vmem_limit_bytes=52 * 1024 * 1024),
        cost_estimate=pl.CostEstimate(
            flops=2 * 1024**3, bytes_accessed=4 * 1024**2, transcendentals=0
        ),
        **kwargs,
    )


def expert_rows(parts, gate_up, down):
    inner = down.shape[0]
    rows = jnp.concatenate([part[...].astype(F32) for part in parts], axis=0).astype(BF16)
    both = dot(rows, gate_up[...])
    start = both.shape[1] // 2
    first, second = both[:, :inner], both[:, start : start + inner]
    return dot((first / (1.0 + jnp.exp(-first)) * second).astype(BF16), down[...])


def rows_kernel(gate_up, down, *refs):
    parts, outs = refs[: len(refs) // 2], refs[len(refs) // 2 :]
    result = expert_rows(parts, gate_up, down)
    size = parts[0].shape[0]
    for k, out in enumerate(outs):
        out[...] = result[k * size : (k + 1) * size].astype(out.dtype)


def dense_in_kernel(columns, tokens, *refs):
    weights, out = refs[:4], refs[4]
    joined = jnp.concatenate([part[:, :columns] for part in weights], axis=0)
    for z in range(4):
        rows = jnp.concatenate([tokens[e, z] for e in range(tokens.shape[0])], axis=0)
        out[z] = dot(rows, joined).astype(BF16)


def late_kernel(part, relay, out):
    out[...] = (part[...] + relay[...].astype(F32)).astype(BF16)


def total_kernel(capacity, place, low, high, *refs):
    sums, outs, whole = refs[:4], refs[4:8], refs[8]
    half = 2 * capacity
    whole[:half] = low[...] + sums[0][...].astype(F32) + sums[1][...].astype(F32)
    whole[half:] = high[...] + sums[2][...].astype(F32) + sums[3][...].astype(F32)
    for k, out in enumerate(outs):
        for j in range(4):

            @pl.when(place[k] == j)
            def _(out=out, j=j):
                out[...] = whole[j * capacity : (j + 1) * capacity].astype(out.dtype)


def in_line_order(parts, axis):
    order = (lax.axis_index(axis) - jnp.arange(4, dtype=jnp.int32)) % 4
    return jnp.stack(parts).at[order].get(mode="promise_in_bounds")


def dense_out_kernel(columns, place, act, *refs):
    weights, out = refs[:4], refs[4]
    contract = (((1,), (1,)), ((), ()))
    for k in range(4):
        part = lax.dot_general(
            act[...], weights[k][:, columns:], contract, preferred_element_type=F32
        ).astype(BF16)
        half = part.shape[0] // 8
        for side in range(2):
            pieces = [part[(2 * j + side) * half : (2 * j + side + 1) * half] for j in range(4)]
            out[2 * place[k] + side] = jnp.concatenate(pieces, axis=0)


def body(
    normed,
    residual,
    expert_index,
    pick_weight,
    dense_gate,
    dense_up,
    dense_down,
    expert_gate,
    expert_up,
    expert_down,
):
    tokens = normed[0]
    picks = expert_index[0]
    weights = pick_weight[0]
    tok_rows, width = tokens.shape
    n_expert = 8
    capacity = min(tok_rows, 9 * tok_rows // (4 * n_expert))
    core = lax.axis_index("core")
    mine = lax.axis_index("x") * 2 + core
    hidden = dense_gate.shape[2]
    slab = width // 4
    step = dense_gate.shape[1]
    piece = width // n_expert

    with jax.named_scope("dispatch"):
        slot = slots_of(picks, n_expert)
        is_mine = picks == mine
        positions = jnp.arange(capacity, dtype=jnp.int32)
        select = jnp.any(
            (positions[:, None, None] == slot[None, :, :]) & is_mine[None, :, :], axis=2
        ).astype(BF16)
        routed = dot(select, tokens).astype(BF16)

    with jax.named_scope("dense_weights"):
        stacked = jnp.concatenate([dense_gate[0], dense_up[0], dense_down[0]], axis=1)
        stacked = after(stacked, routed)
        slabs = [stacked] + [shifted(stacked, "y", by) for by in (1, 2, 3)]
        steps_back = jnp.arange(4, dtype=jnp.int32)
        place_y, place_z = ((lax.axis_index(axis) - steps_back) % 4 for axis in ("y", "z"))

    with jax.named_scope("combine"):
        target = picks * capacity + slot
        columns = jnp.arange(n_expert * capacity, dtype=jnp.int32)
        chosen = jnp.where(columns[None, None, :] == target[:, :, None], weights[:, :, None], 0.0)
        combine = jnp.sum(chosen, axis=1)
        coarse = lax.reduce_precision(combine, 8, 7)
        fine = lax.reduce_precision(combine - coarse, 8, 7)
        coarse, fine = coarse.astype(BF16), fine.astype(BF16)

    down = expert_down[0, 0]
    blank = jnp.zeros((width, -down.shape[0] % 256), BF16)
    gate_up = jnp.concatenate([expert_gate[0, 0], blank, expert_up[0, 0], blank], axis=1)

    half = 2 * capacity
    with jax.named_scope("rows_z"):
        share = tok_rows // n_expert
        own_share = lax.dynamic_slice_in_dim(tokens, mine * share, share, axis=0)
        own_share = own_share.reshape(share, 4, 4, step)
        own_share = own_share.at[:, place_y].get(mode="promise_in_bounds").transpose(2, 0, 1, 3)
        sent = [repeated(routed, 4), own_share.reshape(4, share // 4, width)]
        arrived = exchanged(jnp.concatenate(sent, axis=1), "z")
        line_share = arrived[:, capacity:].reshape(4, share, slab)
        coarse, fine, gate_up = after((coarse, fine, gate_up), routed)
        group = after(arrived, coarse, fine, gate_up, *slabs[1:])[:, :capacity]
        low, high = (block.reshape(half, width) for block in (group[:2], group[2:]))

    with jax.named_scope("rows_y"):
        prev_low, next_low = shifted(low, "y", 1), shifted(low, "y", -1)
        far_low = shifted(prev_low, "y", 1)
        next_high, prev_high = shifted(high, "y", -1), shifted(high, "y", 1)
        far_high = shifted(next_high, "y", -1)

    with jax.named_scope("dense_tokens"):
        line_tokens = exchanged(repeated(line_share, n_expert), EXPERT_AXES)
        line_tokens = after(line_tokens, prev_low, next_low, prev_high, next_high)
        pre = local_call(
            functools.partial(dense_in_kernel, 2 * hidden),
            jax.ShapeDtypeStruct((4, tok_rows, 2 * hidden), BF16),
        )(line_tokens, *slabs)

    half_bf16, half_f32 = (jax.ShapeDtypeStruct(low.shape, dtype) for dtype in (BF16, F32))
    in_smem, in_vmem = (pl.BlockSpec(memory_space=space) for space in (pltpu.SMEM, pltpu.VMEM))
    with jax.named_scope("experts"):
        relay_next, relay_prev, early_next, early_prev, next_part, prev_part = local_call(
            rows_kernel, [half_bf16] * 4 + [half_f32] * 2
        )(gate_up, down, far_low, far_high, next_high, prev_low, next_low, prev_high)

    with jax.named_scope("partials_y"):
        relay_next, relay_prev = shifted(relay_next, "y", 1), shifted(relay_prev, "y", -1)
    with jax.named_scope("dense_hidden"):
        pre = exchanged(pre, "z")
        pre = jnp.sum(pre.astype(F32), axis=0)
        act = swiglu(pre[:, :hidden], pre[:, hidden:])
        line_act = jnp.broadcast_to(act[None], (4,) + act.shape)
    with jax.named_scope("dense_out"):
        half_tokens = tok_rows // 2
        every_act = exchanged(line_act, "z").reshape(4 * tok_rows, hidden)
        by_block = local_call(
            functools.partial(dense_out_kernel, 2 * hidden),
            jax.ShapeDtypeStruct((n_expert, 4 * half_tokens, step), BF16),
            in_specs=[in_smem] + [in_vmem] * 5,
        )(place_y, every_act, *slabs)

    with jax.named_scope("partials_y"):
        early_next, early_prev = shifted(early_next, "y", 1), shifted(early_prev, "y", -1)
        late_next = local_call(late_kernel, half_bf16)(next_part, relay_next)
        late_prev = local_call(late_kernel, half_bf16)(prev_part, relay_prev)
        own_low, own_high = local_call(rows_kernel, [half_f32] * 2)(
            after(gate_up, late_next, late_prev), down, low, high
        )
        late_next, late_prev = shifted(late_next, "y", 1), shifted(late_prev, "y", -1)

    with jax.named_scope("partials_z"):
        rows_f32, rows_bf16 = (jax.ShapeDtypeStruct(routed.shape, dtype) for dtype in (F32, BF16))
        kept_rows, *sent = local_call(
            functools.partial(total_kernel, capacity),
            [rows_f32] + [rows_bf16] * 3,
            in_specs=[in_smem] + [in_vmem] * 6,
            scratch_shapes=[pltpu.VMEM((4 * capacity, width), F32)],
        )(place_z, own_low, own_high, late_next, early_prev, early_next, late_prev)
        recv = [shifted(part, "z", by) for part, by in zip(sent, (-1, -2, -3))]
        expert_out = (kept_rows + sum(part.astype(F32) for part in recv)).astype(BF16)

    with jax.named_scope("dense_out"):
        block_sum = jnp.sum(exchanged(by_block, EXPERT_AXES).astype(F32), axis=0).astype(BF16)
        block_sum = block_sum.reshape(4, half_tokens, step)
        blocks = []
        for by in range(4):
            there = (lax.axis_index("z") + by) % 4
            block = lax.dynamic_index_in_dim(block_sum, there, 0, keepdims=False)
            blocks.append(shifted(block, "z", by) if by else block)
        blocks = in_line_order(blocks, "z")
        kept = lax.dynamic_slice_in_dim(blocks, 2 * core, 2, axis=0)
        given = lax.dynamic_slice_in_dim(blocks, 2 - 2 * core, 2, axis=0)
        taken = shifted(given, "core", 1)
        first = jnp.where(core == 0, kept, taken)
        second = jnp.where(core == 0, taken, kept)
        dense_total = jnp.concatenate([first, second], axis=1).transpose(1, 0, 2)
    base = residual[0].astype(F32) + dense_total.reshape(tok_rows, piece).astype(F32)

    with jax.named_scope("combine"):
        by_feature = expert_out.reshape(capacity, n_expert, piece).transpose(1, 0, 2)
        returned = exchanged(by_feature, EXPERT_AXES).reshape(n_expert * capacity, piece)
        spread = dot(coarse, returned) + dot(fine, returned)
        mixed = (base + spread).astype(BF16)
    with jax.named_scope("next_section"):
        return shifted(mixed, "section", 1)[None]


def solution(mesh):
    fine_mesh = Mesh(mesh.devices.reshape(GRID), AXES)
    data = ("y", "z")
    placed = (
        P("section", data, None),
        P("section", data, EXPERT_AXES),
        P("section", data, None),
        P("section", data, None),
        P("section", data, EXPERT_AXES),
        P("section", data, EXPERT_AXES),
        P("section", data, EXPERT_AXES),
        P("section", EXPERT_AXES, None, data),
        P("section", EXPERT_AXES, None, data),
        P("section", EXPERT_AXES, data, None),
    )
    return jax.shard_map(
        body,
        mesh=fine_mesh,
        in_specs=placed,
        out_specs=P("section", data, EXPERT_AXES),
        check_vma=False,
    )
```

```python
import functools

import jax
import jax.numpy as jnp
from jax import lax
from jax.experimental import pallas as pl
from jax.experimental.pallas import tpu as pltpu
from jax.sharding import Mesh, PartitionSpec as P

AXES = ("section", "y", "z", "x", "core")
GRID = (4, 4, 4, 4, 2)
EXPERT_AXES = ("x", "core")
BF16, F32 = jnp.bfloat16, jnp.float32


def shifted(x, axis, by):
    peers = lax.axis_size(axis)
    return lax.ppermute(x, axis, [(i, (i + by) % peers) for i in range(peers)])


def exchanged(x, axes):
    return lax.all_to_all(x, axes, split_axis=0, concat_axis=0, tiled=True)


def repeated(x, times):
    return jnp.broadcast_to(x[None], (times,) + x.shape)


def after(x, *others):
    return lax.optimization_barrier((x,) + others)[0]


def swiglu(first, second):
    return (jax.nn.silu(first) * second).astype(BF16)


def dot(a, b):
    return jnp.dot(a, b, preferred_element_type=F32)


def slots_of(picks, n_expert):
    labels = jnp.arange(n_expert, dtype=jnp.int32)
    named = (picks[:, :, None] == labels[None, None, :]).astype(jnp.int32)
    per_token = jnp.sum(named, axis=1, dtype=jnp.int32)
    earlier = jnp.cumsum(per_token, axis=0, dtype=jnp.int32) - per_token
    return jnp.sum(named * earlier[:, None, :], axis=2, dtype=jnp.int32)


def local_call(kernel, out_shape, flops=2 * 1024**3, **kwargs):
    return pl.pallas_call(
        kernel,
        out_shape=out_shape,
        compiler_params=pltpu.CompilerParams(vmem_limit_bytes=52 * 1024 * 1024),
        cost_estimate=pl.CostEstimate(
            flops=flops, bytes_accessed=4 * 1024**2, transcendentals=0
        ),
        **kwargs,
    )


def rows_kernel(count, gate_up, down, *refs):
    parts, outs, whole = refs[:count], refs[count : 2 * count], refs[-1]
    start, spans = 0, []
    for part in parts:
        spans.append(slice(start, start + part.shape[0]))
        whole[spans[-1]] = part[...].astype(F32)
        start += part.shape[0]
    inner = down.shape[0]
    both = dot(whole[...].astype(BF16), gate_up[...])
    middle = both.shape[1] // 2
    first, second = both[:, :inner], both[:, middle : middle + inner]
    act = (first / (1.0 + jnp.exp(-first)) * second).astype(BF16)
    whole[...] = dot(act, down[...])
    for span, out in zip(spans, outs):
        out[...] = whole[span].astype(out.dtype)


def rows_and_dense_kernel(count, columns, tokens, *refs):
    weights, rest, pre, whole = refs[:4], refs[4:-2], refs[-2], refs[-1]
    joined = jnp.concatenate([part[:, :columns] for part in weights], axis=0)
    for z in range(4):
        rows = jnp.concatenate([tokens[e, z] for e in range(tokens.shape[0])], axis=0)
        pre[z] = dot(rows, joined).astype(BF16)
    rows_kernel(count, *rest, whole)


def total_kernel(own, one, two, three, *refs):
    outs, whole = refs[:3], refs[3]
    whole[...] = own[...] + (
        one[...].astype(F32) + two[...].astype(F32) + three[...].astype(F32)
    )
    size = outs[0].shape[0]
    for k, out in enumerate(outs):
        out[...] = whole[k * size : (k + 1) * size].astype(out.dtype)


def in_line_order(parts, axis):
    order = (lax.axis_index(axis) - jnp.arange(4, dtype=jnp.int32)) % 4
    return jnp.stack(parts).at[order].get(mode="promise_in_bounds")


def dense_out_kernel(columns, place, act, *refs):
    weights, out = refs[:4], refs[4]
    contract = (((1,), (1,)), ((), ()))
    for k in range(4):
        part = lax.dot_general(
            act[...], weights[k][:, columns:], contract, preferred_element_type=F32
        ).astype(BF16)
        half = part.shape[0] // 8
        for side in range(2):
            pieces = [part[(2 * j + side) * half : (2 * j + side + 1) * half] for j in range(4)]
            out[2 * place[k] + side] = jnp.concatenate(pieces, axis=0)


def body(
    normed,
    residual,
    expert_index,
    pick_weight,
    dense_gate,
    dense_up,
    dense_down,
    expert_gate,
    expert_up,
    expert_down,
):
    tokens = normed[0]
    picks = expert_index[0]
    weights = pick_weight[0]
    tok_rows, width = tokens.shape
    n_expert = 8
    capacity = min(tok_rows, 9 * tok_rows // (4 * n_expert))
    core = lax.axis_index("core")
    mine = lax.axis_index("x") * 2 + core
    hidden = dense_gate.shape[2]
    slab = width // 4
    step = dense_gate.shape[1]
    piece = width // n_expert

    with jax.named_scope("dispatch"):
        slot = slots_of(picks, n_expert)
        is_mine = picks == mine
        positions = jnp.arange(capacity, dtype=jnp.int32)
        select = jnp.any(
            (positions[:, None, None] == slot[None, :, :]) & is_mine[None, :, :], axis=2
        ).astype(BF16)
        routed = dot(select, tokens).astype(BF16)

    with jax.named_scope("dense_weights"):
        stacked = jnp.concatenate([dense_gate[0], dense_up[0], dense_down[0]], axis=1)
        stacked = after(stacked, routed)
        slabs = [stacked] + [shifted(stacked, "y", by) for by in (1, 2, 3)]
        steps_back = jnp.arange(4, dtype=jnp.int32)
        place_y, place_z = ((lax.axis_index(axis) - steps_back) % 4 for axis in ("y", "z"))

    with jax.named_scope("combine"):
        target = picks * capacity + slot
        columns = jnp.arange(n_expert * capacity, dtype=jnp.int32)
        chosen = jnp.where(columns[None, None, :] == target[:, :, None], weights[:, :, None], 0.0)
        combine = jnp.sum(chosen, axis=1)
        coarse = lax.reduce_precision(combine, 8, 7)
        fine = lax.reduce_precision(combine - coarse, 8, 7)
        coarse, fine = coarse.astype(BF16), fine.astype(BF16)

    down = expert_down[0, 0]
    blank = jnp.zeros((width, -down.shape[0] % 256), BF16)
    gate_up = jnp.concatenate([expert_gate[0, 0], blank, expert_up[0, 0], blank], axis=1)

    half = 2 * capacity
    with jax.named_scope("rows_z"):
        share = tok_rows // n_expert
        own_share = lax.dynamic_slice_in_dim(tokens, mine * share, share, axis=0)
        own_share = own_share.reshape(share, 4, 4, step)
        own_share = own_share.at[:, place_y].get(mode="promise_in_bounds").transpose(2, 0, 1, 3)
        sent = [repeated(routed, 4), own_share.reshape(4, share // 4, width)]
        arrived = exchanged(jnp.concatenate(sent, axis=1), "z")
        line_share = arrived[:, capacity:].reshape(4, share, slab)
        coarse, fine, gate_up = after((coarse, fine, gate_up), routed)

    around = (1, -1, 2)
    with jax.named_scope("rows_y"):
        own_rows = [shifted(routed, "y", by) for by in around]
        line = after(arrived, coarse, fine, gate_up, slabs[1], slabs[3], *own_rows)[:, :capacity]
        line = line.at[place_z[1:]].get(mode="promise_in_bounds").reshape(3 * capacity, width)
        line_rows = [shifted(line, "y", by) for by in around]

    with jax.named_scope("dense_tokens"):
        line_tokens = exchanged(repeated(line_share, n_expert), EXPERT_AXES)

    def held(like, dtype):
        return jax.ShapeDtypeStruct(like.shape, dtype)

    with jax.named_scope("experts"):
        *parts, pre = local_call(
            functools.partial(rows_and_dense_kernel, 6, 2 * hidden),
            [held(line, BF16)] * 3
            + [held(routed, BF16)] * 3
            + [jax.ShapeDtypeStruct((4, tok_rows, 2 * hidden), BF16)],
            scratch_shapes=[pltpu.VMEM((12 * capacity, width), F32)],
        )(line_tokens, *slabs, gate_up, down, *line_rows, *own_rows)
    with jax.named_scope("partials_y"):
        line_back = [shifted(part, "y", -by) for part, by in zip(parts[:3], around)]
        own_back = [shifted(part, "y", -by) for part, by in zip(parts[3:], around)]

    with jax.named_scope("dense_hidden"):
        pre = exchanged(pre, "z")
        pre = jnp.sum(pre.astype(F32), axis=0)
        act = swiglu(pre[:, :hidden], pre[:, hidden:])
        line_act = jnp.broadcast_to(act[None], (4,) + act.shape)
    with jax.named_scope("dense_out"):
        half_tokens = tok_rows // 2
        every_act = exchanged(line_act, "z").reshape(4 * tok_rows, hidden)
        by_block = local_call(
            functools.partial(dense_out_kernel, 2 * hidden),
            jax.ShapeDtypeStruct((n_expert, 4 * half_tokens, step), BF16),
            in_specs=[pl.BlockSpec(memory_space=pltpu.SMEM)]
            + [pl.BlockSpec(memory_space=pltpu.VMEM)] * 5,
        )(place_y, every_act, *slabs)

    with jax.named_scope("experts"):
        line_part, own_part = local_call(
            functools.partial(rows_kernel, 2),
            [held(line, F32), held(routed, F32)],
            scratch_shapes=[pltpu.VMEM((4 * capacity, width), F32)],
        )(after(gate_up, parts[0]), down, line, routed)
    with jax.named_scope("partials_z"):
        sent = local_call(
            total_kernel,
            [held(routed, BF16)] * 3,
            flops=200 * 1024**3,
            scratch_shapes=[pltpu.VMEM((3 * capacity, width), F32)],
        )(line_part, *line_back)
        recv = [shifted(part, "z", by) for part, by in zip(sent, (-1, -2, -3))]
        expert_out = (own_part + sum(part.astype(F32) for part in own_back + recv)).astype(BF16)

    with jax.named_scope("dense_out"):
        block_sum = jnp.sum(exchanged(by_block, EXPERT_AXES).astype(F32), axis=0).astype(BF16)
        block_sum = block_sum.reshape(4, half_tokens, step)
        blocks = []
        for by in range(4):
            there = (lax.axis_index("z") + by) % 4
            block = lax.dynamic_index_in_dim(block_sum, there, 0, keepdims=False)
            blocks.append(shifted(block, "z", by) if by else block)
        blocks = in_line_order(blocks, "z")
        kept = lax.dynamic_slice_in_dim(blocks, 2 * core, 2, axis=0)
        given = lax.dynamic_slice_in_dim(blocks, 2 - 2 * core, 2, axis=0)
        taken = shifted(given, "core", 1)
        first = jnp.where(core == 0, kept, taken)
        second = jnp.where(core == 0, taken, kept)
        dense_total = jnp.concatenate([first, second], axis=1).transpose(1, 0, 2)
    base = residual[0].astype(F32) + dense_total.reshape(tok_rows, piece).astype(F32)

    with jax.named_scope("combine"):
        by_feature = expert_out.reshape(capacity, n_expert, piece).transpose(1, 0, 2)
        returned = exchanged(by_feature, EXPERT_AXES).reshape(n_expert * capacity, piece)
        spread = dot(coarse, returned) + dot(fine, returned)
        mixed = (base + spread).astype(BF16)
    with jax.named_scope("next_section"):
        return shifted(mixed, "section", 1)[None]


def solution(mesh):
    fine_mesh = Mesh(mesh.devices.reshape(GRID), AXES)
    data = ("y", "z")
    placed = (
        P("section", data, None),
        P("section", data, EXPERT_AXES),
        P("section", data, None),
        P("section", data, None),
        P("section", data, EXPERT_AXES),
        P("section", data, EXPERT_AXES),
        P("section", data, EXPERT_AXES),
        P("section", EXPERT_AXES, None, data),
        P("section", EXPERT_AXES, None, data),
        P("section", EXPERT_AXES, data, None),
    )
    return jax.shard_map(
        body,
        mesh=fine_mesh,
        in_specs=placed,
        out_specs=P("section", data, EXPERT_AXES),
        check_vma=False,
    )
```

```python
import functools

import jax
import jax.numpy as jnp
from jax import lax
from jax.experimental import pallas as pl
from jax.experimental.pallas import tpu as pltpu
from jax.sharding import Mesh, PartitionSpec as P

AXES = ("section", "y", "z", "x", "core")
GRID = (4, 4, 4, 4, 2)
EXPERT_AXES = ("x", "core")
BF16, F32 = jnp.bfloat16, jnp.float32
LONG = 100 * 1024**3


def shifted(x, axis, by):
    peers = lax.axis_size(axis)
    return lax.ppermute(x, axis, [(i, (i + by) % peers) for i in range(peers)])


def exchanged(x, axes):
    return lax.all_to_all(x, axes, split_axis=0, concat_axis=0, tiled=True)


def repeated(x, times):
    return jnp.broadcast_to(x[None], (times,) + x.shape)


def after(x, *others):
    return lax.optimization_barrier((x,) + others)[0]


def swiglu(first, second):
    return (jax.nn.silu(first) * second).astype(BF16)


def dot(a, b):
    return jnp.dot(a, b, preferred_element_type=F32)


def slots_of(picks, n_expert):
    labels = jnp.arange(n_expert, dtype=jnp.int32)
    named = (picks[:, :, None] == labels[None, None, :]).astype(jnp.int32)
    per_token = jnp.sum(named, axis=1, dtype=jnp.int32)
    earlier = jnp.cumsum(per_token, axis=0, dtype=jnp.int32) - per_token
    return jnp.sum(named * earlier[:, None, :], axis=2, dtype=jnp.int32)


def local_call(kernel, out_shape, flops=2 * 1024**3, **kwargs):
    return pl.pallas_call(
        kernel,
        out_shape=out_shape,
        compiler_params=pltpu.CompilerParams(vmem_limit_bytes=52 * 1024 * 1024),
        cost_estimate=pl.CostEstimate(
            flops=flops, bytes_accessed=4 * 1024**2, transcendentals=0
        ),
        **kwargs,
    )


def expert_rows(parts, gate_up, down):
    inner = down.shape[0]
    rows = jnp.concatenate([part[...].astype(F32) for part in parts], axis=0).astype(BF16)
    both = dot(rows, gate_up[...])
    start = both.shape[1] // 2
    first, second = both[:, :inner], both[:, start : start + inner]
    return dot((first / (1.0 + jnp.exp(-first)) * second).astype(BF16), down[...])


def rows_kernel(gate_up, down, *refs):
    parts, outs = refs[: len(refs) // 2], refs[len(refs) // 2 :]
    result = expert_rows(parts, gate_up, down)
    size = parts[0].shape[0]
    for k, out in enumerate(outs):
        out[...] = result[k * size : (k + 1) * size].astype(out.dtype)


def dense_in_kernel(columns, tokens, *refs):
    weights, out = refs[:4], refs[4]
    joined = jnp.concatenate([part[:, :columns] for part in weights], axis=0)
    for z in range(4):
        rows = jnp.concatenate([tokens[e, z] for e in range(tokens.shape[0])], axis=0)
        out[z] = dot(rows, joined).astype(BF16)


def late_kernel(part_next, part_prev, relay_next, relay_prev, to_next, to_prev):
    to_next[...] = (part_next[...] + relay_next[...].astype(F32)).astype(BF16)
    to_prev[...] = (part_prev[...] + relay_prev[...].astype(F32)).astype(BF16)


def total_kernel(capacity, place, low, high, *refs):
    sums, outs, whole = refs[:4], refs[4:8], refs[8]
    half = 2 * capacity
    whole[:half] = low[...] + sums[0][...].astype(F32) + sums[1][...].astype(F32)
    whole[half:] = high[...] + sums[2][...].astype(F32) + sums[3][...].astype(F32)
    for k, out in enumerate(outs):
        for j in range(4):

            @pl.when(place[k] == j)
            def _(out=out, j=j):
                out[...] = whole[j * capacity : (j + 1) * capacity].astype(out.dtype)


def in_line_order(parts, axis):
    order = (lax.axis_index(axis) - jnp.arange(4, dtype=jnp.int32)) % 4
    return jnp.stack(parts).at[order].get(mode="promise_in_bounds")


def dense_out_kernel(columns, place, act, *refs):
    weights, out = refs[:4], refs[4]
    contract = (((1,), (1,)), ((), ()))
    for k in range(4):
        part = lax.dot_general(
            act[...], weights[k][:, columns:], contract, preferred_element_type=F32
        ).astype(BF16)
        half = part.shape[0] // 8
        for side in range(2):
            pieces = [part[(2 * j + side) * half : (2 * j + side + 1) * half] for j in range(4)]
            out[2 * place[k] + side] = jnp.concatenate(pieces, axis=0)


def body(
    normed,
    residual,
    expert_index,
    pick_weight,
    dense_gate,
    dense_up,
    dense_down,
    expert_gate,
    expert_up,
    expert_down,
):
    tokens = normed[0]
    picks = expert_index[0]
    weights = pick_weight[0]
    tok_rows, width = tokens.shape
    n_expert = 8
    capacity = min(tok_rows, 9 * tok_rows // (4 * n_expert))
    core = lax.axis_index("core")
    mine = lax.axis_index("x") * 2 + core
    hidden = dense_gate.shape[2]
    slab = width // 4
    step = dense_gate.shape[1]
    piece = width // n_expert

    with jax.named_scope("dispatch"):
        slot = slots_of(picks, n_expert)
        is_mine = picks == mine
        positions = jnp.arange(capacity, dtype=jnp.int32)
        select = jnp.any(
            (positions[:, None, None] == slot[None, :, :]) & is_mine[None, :, :], axis=2
        ).astype(BF16)
        routed = dot(select, tokens).astype(BF16)

    with jax.named_scope("dense_weights"):
        stacked = jnp.concatenate([dense_gate[0], dense_up[0], dense_down[0]], axis=1)
        stacked = after(stacked, routed)
        slabs = [stacked] + [shifted(stacked, "y", by) for by in (1, 2, 3)]
        steps_back = jnp.arange(4, dtype=jnp.int32)
        place_y, place_z = ((lax.axis_index(axis) - steps_back) % 4 for axis in ("y", "z"))

    with jax.named_scope("combine"):
        target = picks * capacity + slot
        columns = jnp.arange(n_expert * capacity, dtype=jnp.int32)
        chosen = jnp.where(columns[None, None, :] == target[:, :, None], weights[:, :, None], 0.0)
        combine = jnp.sum(chosen, axis=1)
        coarse = lax.reduce_precision(combine, 8, 7)
        fine = lax.reduce_precision(combine - coarse, 8, 7)
        coarse, fine = coarse.astype(BF16), fine.astype(BF16)

    down = expert_down[0, 0]
    blank = jnp.zeros((width, -down.shape[0] % 256), BF16)
    gate_up = jnp.concatenate([expert_gate[0, 0], blank, expert_up[0, 0], blank], axis=1)

    half = 2 * capacity
    with jax.named_scope("rows_z"):
        share = tok_rows // n_expert
        own_share = lax.dynamic_slice_in_dim(tokens, mine * share, share, axis=0)
        own_share = own_share.reshape(share, 4, 4, step)
        own_share = own_share.at[:, place_y].get(mode="promise_in_bounds").transpose(2, 0, 1, 3)
        sent = [repeated(routed, 4), own_share.reshape(4, share // 4, width)]
        arrived = exchanged(jnp.concatenate(sent, axis=1), "z")
        line_share = arrived[:, capacity:].reshape(4, share, slab)
        coarse, fine, gate_up = after((coarse, fine, gate_up), routed)
        group = after(arrived, coarse, fine, gate_up, *slabs[1:])[:, :capacity]
        low, high = (block.reshape(half, width) for block in (group[:2], group[2:]))

    with jax.named_scope("rows_y"):
        prev_low, next_low = shifted(low, "y", 1), shifted(low, "y", -1)
        far_low = shifted(prev_low, "y", 1)
        next_high, prev_high = shifted(high, "y", -1), shifted(high, "y", 1)
        far_high = shifted(next_high, "y", -1)

    with jax.named_scope("dense_tokens"):
        line_tokens = exchanged(repeated(line_share, n_expert), EXPERT_AXES)
        pre = local_call(
            functools.partial(dense_in_kernel, 2 * hidden),
            jax.ShapeDtypeStruct((4, tok_rows, 2 * hidden), BF16),
        )(line_tokens, *slabs)

    half_bf16, half_f32 = (jax.ShapeDtypeStruct(low.shape, dtype) for dtype in (BF16, F32))
    in_smem, in_vmem = (pl.BlockSpec(memory_space=space) for space in (pltpu.SMEM, pltpu.VMEM))
    with jax.named_scope("experts"):
        relay_next, relay_prev, early_next, early_prev, next_part, prev_part = local_call(
            rows_kernel, [half_bf16] * 4 + [half_f32] * 2, LONG
        )(gate_up, down, far_low, far_high, next_high, prev_low, next_low, prev_high)

    with jax.named_scope("partials_y"):
        relay_next, relay_prev = shifted(relay_next, "y", 1), shifted(relay_prev, "y", -1)
    with jax.named_scope("dense_hidden"):
        pre = exchanged(pre, "z")
        pre = jnp.sum(pre.astype(F32), axis=0)
        act = swiglu(pre[:, :hidden], pre[:, hidden:])
        line_act = jnp.broadcast_to(act[None], (4,) + act.shape)
    with jax.named_scope("dense_out"):
        half_tokens = tok_rows // 2
        every_act = exchanged(line_act, "z").reshape(4 * tok_rows, hidden)
        by_block = local_call(
            functools.partial(dense_out_kernel, 2 * hidden),
            jax.ShapeDtypeStruct((n_expert, 4 * half_tokens, step), BF16),
            in_specs=[in_smem] + [in_vmem] * 5,
        )(place_y, every_act, *slabs)

    with jax.named_scope("partials_y"):
        early_next, early_prev = shifted(early_next, "y", 1), shifted(early_prev, "y", -1)
        late_next, late_prev = local_call(late_kernel, [half_bf16] * 2, LONG)(
            next_part, prev_part, relay_next, relay_prev
        )
        own_low, own_high = local_call(rows_kernel, [half_f32] * 2)(
            after(gate_up, late_next, late_prev), down, low, high
        )
        late_next, late_prev = shifted(late_next, "y", 1), shifted(late_prev, "y", -1)

    with jax.named_scope("partials_z"):
        rows_f32, rows_bf16 = (jax.ShapeDtypeStruct(routed.shape, dtype) for dtype in (F32, BF16))
        kept_rows, *sent = local_call(
            functools.partial(total_kernel, capacity),
            [rows_f32] + [rows_bf16] * 3,
            in_specs=[in_smem] + [in_vmem] * 6,
            scratch_shapes=[pltpu.VMEM((4 * capacity, width), F32)],
        )(place_z, own_low, own_high, late_next, early_prev, early_next, late_prev)
        recv = [shifted(part, "z", by) for part, by in zip(sent, (-1, -2, -3))]
        expert_out = (kept_rows + sum(part.astype(F32) for part in recv)).astype(BF16)

    with jax.named_scope("dense_out"):
        block_sum = jnp.sum(exchanged(by_block, EXPERT_AXES).astype(F32), axis=0).astype(BF16)
        block_sum = block_sum.reshape(4, half_tokens, step)
        blocks = []
        for by in range(4):
            there = (lax.axis_index("z") + by) % 4
            block = lax.dynamic_index_in_dim(block_sum, there, 0, keepdims=False)
            blocks.append(shifted(block, "z", by) if by else block)
        blocks = in_line_order(blocks, "z")
        kept = lax.dynamic_slice_in_dim(blocks, 2 * core, 2, axis=0)
        given = lax.dynamic_slice_in_dim(blocks, 2 - 2 * core, 2, axis=0)
        taken = shifted(given, "core", 1)
        first = jnp.where(core == 0, kept, taken)
        second = jnp.where(core == 0, taken, kept)
        dense_total = jnp.concatenate([first, second], axis=1).transpose(1, 0, 2)
    base = residual[0].astype(F32) + dense_total.reshape(tok_rows, piece).astype(F32)

    with jax.named_scope("combine"):
        by_feature = expert_out.reshape(capacity, n_expert, piece).transpose(1, 0, 2)
        returned = exchanged(by_feature, EXPERT_AXES).reshape(n_expert * capacity, piece)
        spread = dot(coarse, returned) + dot(fine, returned)
        mixed = (base + spread).astype(BF16)
    with jax.named_scope("next_section"):
        return shifted(mixed, "section", 1)[None]


def solution(mesh):
    fine_mesh = Mesh(mesh.devices.reshape(GRID), AXES)
    data = ("y", "z")
    placed = (
        P("section", data, None),
        P("section", data, EXPERT_AXES),
        P("section", data, None),
        P("section", data, None),
        P("section", data, EXPERT_AXES),
        P("section", data, EXPERT_AXES),
        P("section", data, EXPERT_AXES),
        P("section", EXPERT_AXES, None, data),
        P("section", EXPERT_AXES, None, data),
        P("section", EXPERT_AXES, data, None),
    )
    return jax.shard_map(
        body,
        mesh=fine_mesh,
        in_specs=placed,
        out_specs=P("section", data, EXPERT_AXES),
        check_vma=False,
    )
```

```python
import functools

import jax
import jax.numpy as jnp
from jax import lax
from jax.experimental import pallas as pl
from jax.experimental.pallas import tpu as pltpu
from jax.sharding import Mesh, PartitionSpec as P

AXES = ("section", "y", "z", "x", "core")
GRID = (4, 4, 4, 4, 2)
EXPERT_AXES = ("x", "core")
BF16, F32 = jnp.bfloat16, jnp.float32
LONG = 100 * 1024**3


def shifted(x, axis, by):
    peers = lax.axis_size(axis)
    return lax.ppermute(x, axis, [(i, (i + by) % peers) for i in range(peers)])


def exchanged(x, axes):
    return lax.all_to_all(x, axes, split_axis=0, concat_axis=0, tiled=True)


def repeated(x, times):
    return jnp.broadcast_to(x[None], (times,) + x.shape)


def after(x, *others):
    return lax.optimization_barrier((x,) + others)[0]


def swiglu(first, second):
    return (jax.nn.silu(first) * second).astype(BF16)


def dot(a, b):
    return jnp.dot(a, b, preferred_element_type=F32)


def slots_of(picks, n_expert):
    labels = jnp.arange(n_expert, dtype=jnp.int32)
    named = (picks[:, :, None] == labels[None, None, :]).astype(jnp.int32)
    per_token = jnp.sum(named, axis=1, dtype=jnp.int32)
    earlier = jnp.cumsum(per_token, axis=0, dtype=jnp.int32) - per_token
    return jnp.sum(named * earlier[:, None, :], axis=2, dtype=jnp.int32)


def local_call(kernel, out_shape, flops=2 * 1024**3, **kwargs):
    return pl.pallas_call(
        kernel,
        out_shape=out_shape,
        compiler_params=pltpu.CompilerParams(vmem_limit_bytes=52 * 1024 * 1024),
        cost_estimate=pl.CostEstimate(
            flops=flops, bytes_accessed=4 * 1024**2, transcendentals=0
        ),
        **kwargs,
    )


def expert_rows(parts, gate_up, down):
    inner = down.shape[0]
    rows = jnp.concatenate([part[...].astype(F32) for part in parts], axis=0).astype(BF16)
    both = dot(rows, gate_up[...])
    start = both.shape[1] // 2
    first, second = both[:, :inner], both[:, start : start + inner]
    return dot((first / (1.0 + jnp.exp(-first)) * second).astype(BF16), down[...])


def rows_kernel(gate_up, down, *refs):
    parts, outs = refs[: len(refs) // 2], refs[len(refs) // 2 :]
    result = expert_rows(parts, gate_up, down)
    size = parts[0].shape[0]
    for k, out in enumerate(outs):
        out[...] = result[k * size : (k + 1) * size].astype(out.dtype)


def dense_in_kernel(columns, tokens, *refs):
    weights, out = refs[:4], refs[4]
    joined = jnp.concatenate([part[:, :columns] for part in weights], axis=0)
    for z in range(4):
        rows = jnp.concatenate([tokens[e, z] for e in range(tokens.shape[0])], axis=0)
        out[z] = dot(rows, joined).astype(BF16)


def late_kernel(part_next, part_prev, relay_next, relay_prev, to_next, to_prev):
    to_next[...] = (part_next[...] + relay_next[...].astype(F32)).astype(BF16)
    to_prev[...] = (part_prev[...] + relay_prev[...].astype(F32)).astype(BF16)


def total_kernel(capacity, place, low, high, *refs):
    sums, outs, whole = refs[:4], refs[4:8], refs[8]
    half = 2 * capacity
    whole[:half] = low[...] + sums[0][...].astype(F32) + sums[1][...].astype(F32)
    whole[half:] = high[...] + sums[2][...].astype(F32) + sums[3][...].astype(F32)
    for k, out in enumerate(outs):
        for j in range(4):

            @pl.when(place[k] == j)
            def _(out=out, j=j):
                out[...] = whole[j * capacity : (j + 1) * capacity].astype(out.dtype)


def unpack_kernel(capacity, arrived, low, high, tokens, rows, share):
    half = low.shape[0] // capacity
    for first, out in ((0, low), (half, high)):
        for k in range(half):
            block = arrived[first + k].astype(F32)
            rows[k * capacity : (k + 1) * capacity] = block[:capacity]
        out[...] = rows[...].astype(BF16)
    width = tokens.shape[3]
    for z in range(tokens.shape[1]):
        block = arrived[z].astype(F32)
        for r in range(tokens.shape[2] // 4):
            for j in range(4):
                share[4 * r + j : 4 * r + j + 1] = block[
                    capacity + r : capacity + r + 1, j * width : (j + 1) * width
                ]
        value = share[...].astype(BF16)
        for e in range(tokens.shape[0]):
            tokens[e, z] = value


def in_line_order(parts, axis):
    order = (lax.axis_index(axis) - jnp.arange(4, dtype=jnp.int32)) % 4
    return jnp.stack(parts).at[order].get(mode="promise_in_bounds")


def dense_out_kernel(columns, place, act, *refs):
    weights, out = refs[:4], refs[4]
    contract = (((1,), (1,)), ((), ()))
    for k in range(4):
        part = lax.dot_general(
            act[...], weights[k][:, columns:], contract, preferred_element_type=F32
        ).astype(BF16)
        half = part.shape[0] // 8
        for side in range(2):
            pieces = [part[(2 * j + side) * half : (2 * j + side + 1) * half] for j in range(4)]
            out[2 * place[k] + side] = jnp.concatenate(pieces, axis=0)


def body(
    normed,
    residual,
    expert_index,
    pick_weight,
    dense_gate,
    dense_up,
    dense_down,
    expert_gate,
    expert_up,
    expert_down,
):
    tokens = normed[0]
    picks = expert_index[0]
    weights = pick_weight[0]
    tok_rows, width = tokens.shape
    n_expert = 8
    capacity = min(tok_rows, 9 * tok_rows // (4 * n_expert))
    core = lax.axis_index("core")
    mine = lax.axis_index("x") * 2 + core
    hidden = dense_gate.shape[2]
    slab = width // 4
    step = dense_gate.shape[1]
    piece = width // n_expert

    with jax.named_scope("dispatch"):
        slot = slots_of(picks, n_expert)
        is_mine = picks == mine
        positions = jnp.arange(capacity, dtype=jnp.int32)
        select = jnp.any(
            (positions[:, None, None] == slot[None, :, :]) & is_mine[None, :, :], axis=2
        ).astype(BF16)
        routed = dot(select, tokens).astype(BF16)

    with jax.named_scope("dense_weights"):
        stacked = jnp.concatenate([dense_gate[0], dense_up[0], dense_down[0]], axis=1)
        stacked = after(stacked, routed)
        slabs = [stacked] + [shifted(stacked, "y", by) for by in (1, 2, 3)]
        steps_back = jnp.arange(4, dtype=jnp.int32)
        place_y, place_z = ((lax.axis_index(axis) - steps_back) % 4 for axis in ("y", "z"))

    with jax.named_scope("combine"):
        target = picks * capacity + slot
        columns = jnp.arange(n_expert * capacity, dtype=jnp.int32)
        chosen = jnp.where(columns[None, None, :] == target[:, :, None], weights[:, :, None], 0.0)
        combine = jnp.sum(chosen, axis=1)
        coarse = lax.reduce_precision(combine, 8, 7)
        fine = lax.reduce_precision(combine - coarse, 8, 7)
        coarse, fine = coarse.astype(BF16), fine.astype(BF16)

    down = expert_down[0, 0]
    blank = jnp.zeros((width, -down.shape[0] % 256), BF16)
    gate_up = jnp.concatenate([expert_gate[0, 0], blank, expert_up[0, 0], blank], axis=1)

    half = 2 * capacity
    with jax.named_scope("rows_z"):
        share = tok_rows // n_expert
        own_share = lax.dynamic_slice_in_dim(tokens, mine * share, share, axis=0)
        own_share = own_share.reshape(share, 4, 4, step)
        own_share = own_share.at[:, place_y].get(mode="promise_in_bounds").transpose(2, 0, 1, 3)
        sent = [repeated(routed, 4), own_share.reshape(4, share // 4, width)]
        arrived = exchanged(jnp.concatenate(sent, axis=1), "z")
        coarse, fine, gate_up = after((coarse, fine, gate_up), routed)
        low, high, line_tokens = local_call(
            functools.partial(unpack_kernel, capacity),
            [jax.ShapeDtypeStruct((half, width), BF16)] * 2
            + [jax.ShapeDtypeStruct((n_expert, 4, share, slab), BF16)],
            scratch_shapes=[pltpu.VMEM((half, width), F32), pltpu.VMEM((share, slab), F32)],
        )(after(arrived, coarse, fine, gate_up, *slabs[1:]))

    with jax.named_scope("rows_y"):
        prev_low, next_low = shifted(low, "y", 1), shifted(low, "y", -1)
        far_low = shifted(prev_low, "y", 1)
        next_high, prev_high = shifted(high, "y", -1), shifted(high, "y", 1)
        far_high = shifted(next_high, "y", -1)

    with jax.named_scope("dense_tokens"):
        line_tokens = exchanged(line_tokens, EXPERT_AXES)
        pre = local_call(
            functools.partial(dense_in_kernel, 2 * hidden),
            jax.ShapeDtypeStruct((4, tok_rows, 2 * hidden), BF16),
        )(line_tokens, *slabs)

    half_bf16, half_f32 = (jax.ShapeDtypeStruct(low.shape, dtype) for dtype in (BF16, F32))
    in_smem, in_vmem = (pl.BlockSpec(memory_space=space) for space in (pltpu.SMEM, pltpu.VMEM))
    with jax.named_scope("experts"):
        relay_next, relay_prev, early_next, early_prev, next_part, prev_part = local_call(
            rows_kernel, [half_bf16] * 4 + [half_f32] * 2, LONG
        )(gate_up, down, far_low, far_high, next_high, prev_low, next_low, prev_high)

    with jax.named_scope("partials_y"):
        relay_next, relay_prev = shifted(relay_next, "y", 1), shifted(relay_prev, "y", -1)
    with jax.named_scope("dense_hidden"):
        pre = exchanged(pre, "z")
        pre = jnp.sum(pre.astype(F32), axis=0)
        act = swiglu(pre[:, :hidden], pre[:, hidden:])
        line_act = jnp.broadcast_to(act[None], (4,) + act.shape)
    with jax.named_scope("dense_out"):
        half_tokens = tok_rows // 2
        every_act = exchanged(line_act, "z").reshape(4 * tok_rows, hidden)
        by_block = local_call(
            functools.partial(dense_out_kernel, 2 * hidden),
            jax.ShapeDtypeStruct((n_expert, 4 * half_tokens, step), BF16),
            in_specs=[in_smem] + [in_vmem] * 5,
        )(place_y, every_act, *slabs)

    with jax.named_scope("partials_y"):
        early_next, early_prev = shifted(early_next, "y", 1), shifted(early_prev, "y", -1)
        late_next, late_prev = local_call(late_kernel, [half_bf16] * 2, LONG)(
            next_part, prev_part, relay_next, relay_prev
        )
        own_low, own_high = local_call(rows_kernel, [half_f32] * 2)(
            after(gate_up, late_next, late_prev), down, low, high
        )
        late_next, late_prev = shifted(late_next, "y", 1), shifted(late_prev, "y", -1)

    with jax.named_scope("partials_z"):
        rows_f32, rows_bf16 = (jax.ShapeDtypeStruct(routed.shape, dtype) for dtype in (F32, BF16))
        kept_rows, *sent = local_call(
            functools.partial(total_kernel, capacity),
            [rows_f32] + [rows_bf16] * 3,
            in_specs=[in_smem] + [in_vmem] * 6,
            scratch_shapes=[pltpu.VMEM((4 * capacity, width), F32)],
        )(place_z, after(own_low, by_block), own_high, late_next, early_prev, early_next, late_prev)
        recv = [shifted(part, "z", by) for part, by in zip(sent, (-1, -2, -3))]
        expert_out = (kept_rows + sum(part.astype(F32) for part in recv)).astype(BF16)

    with jax.named_scope("dense_out"):
        block_sum = jnp.sum(exchanged(by_block, EXPERT_AXES).astype(F32), axis=0).astype(BF16)
        block_sum = block_sum.reshape(4, half_tokens, step)
        blocks = []
        for by in range(4):
            there = (lax.axis_index("z") + by) % 4
            block = lax.dynamic_index_in_dim(block_sum, there, 0, keepdims=False)
            blocks.append(shifted(block, "z", by) if by else block)
        blocks = in_line_order(blocks, "z")
        kept = lax.dynamic_slice_in_dim(blocks, 2 * core, 2, axis=0)
        given = lax.dynamic_slice_in_dim(blocks, 2 - 2 * core, 2, axis=0)
        taken = shifted(given, "core", 1)
        first = jnp.where(core == 0, kept, taken)
        second = jnp.where(core == 0, taken, kept)
        dense_total = jnp.concatenate([first, second], axis=1).transpose(1, 0, 2)
    base = residual[0].astype(F32) + dense_total.reshape(tok_rows, piece).astype(F32)

    with jax.named_scope("combine"):
        by_feature = expert_out.reshape(capacity, n_expert, piece).transpose(1, 0, 2)
        returned = exchanged(by_feature, EXPERT_AXES).reshape(n_expert * capacity, piece)
        spread = dot(coarse, returned) + dot(fine, returned)
        mixed = (base + spread).astype(BF16)
    with jax.named_scope("next_section"):
        return shifted(mixed, "section", 1)[None]


def solution(mesh):
    fine_mesh = Mesh(mesh.devices.reshape(GRID), AXES)
    data = ("y", "z")
    placed = (
        P("section", data, None),
        P("section", data, EXPERT_AXES),
        P("section", data, None),
        P("section", data, None),
        P("section", data, EXPERT_AXES),
        P("section", data, EXPERT_AXES),
        P("section", data, EXPERT_AXES),
        P("section", EXPERT_AXES, None, data),
        P("section", EXPERT_AXES, None, data),
        P("section", EXPERT_AXES, data, None),
    )
    return jax.shard_map(
        body,
        mesh=fine_mesh,
        in_specs=placed,
        out_specs=P("section", data, EXPERT_AXES),
        check_vma=False,
    )
```

```python
import functools

import jax
import jax.numpy as jnp
from jax import lax
from jax.experimental import pallas as pl
from jax.experimental.pallas import tpu as pltpu
from jax.sharding import Mesh, PartitionSpec as P

AXES = ("section", "y", "z", "x", "core")
GRID = (4, 4, 4, 4, 2)
EXPERT_AXES = ("x", "core")
BF16, F32 = jnp.bfloat16, jnp.float32
LONG = 100 * 1024**3


def shifted(x, axis, by):
    peers = lax.axis_size(axis)
    return lax.ppermute(x, axis, [(i, (i + by) % peers) for i in range(peers)])


def exchanged(x, axes):
    return lax.all_to_all(x, axes, split_axis=0, concat_axis=0, tiled=True)


def repeated(x, times):
    return jnp.broadcast_to(x[None], (times,) + x.shape)


def after(x, *others):
    return lax.optimization_barrier((x,) + others)[0]


def swiglu(first, second):
    return (jax.nn.silu(first) * second).astype(BF16)


def dot(a, b):
    return jnp.dot(a, b, preferred_element_type=F32)


def slots_of(picks, n_expert):
    labels = jnp.arange(n_expert, dtype=jnp.int32)
    named = (picks[:, :, None] == labels[None, None, :]).astype(jnp.int32)
    per_token = jnp.sum(named, axis=1, dtype=jnp.int32)
    earlier = jnp.cumsum(per_token, axis=0, dtype=jnp.int32) - per_token
    return jnp.sum(named * earlier[:, None, :], axis=2, dtype=jnp.int32)


def local_call(kernel, out_shape, flops=2 * 1024**3, **kwargs):
    return pl.pallas_call(
        kernel,
        out_shape=out_shape,
        compiler_params=pltpu.CompilerParams(vmem_limit_bytes=52 * 1024 * 1024),
        cost_estimate=pl.CostEstimate(
            flops=flops, bytes_accessed=4 * 1024**2, transcendentals=0
        ),
        **kwargs,
    )


def expert_rows(parts, gate_up, down):
    inner = down.shape[0]
    rows = jnp.concatenate([part[...].astype(F32) for part in parts], axis=0).astype(BF16)
    both = dot(rows, gate_up[...])
    start = both.shape[1] // 2
    first, second = both[:, :inner], both[:, start : start + inner]
    return dot((first / (1.0 + jnp.exp(-first)) * second).astype(BF16), down[...])


def rows_kernel(gate_up, down, *refs):
    parts, outs = refs[: len(refs) // 2], refs[len(refs) // 2 :]
    result = expert_rows(parts, gate_up, down)
    size = parts[0].shape[0]
    for k, out in enumerate(outs):
        out[...] = result[k * size : (k + 1) * size].astype(out.dtype)


def dense_in_kernel(columns, tokens, *refs):
    weights, out = refs[:4], refs[4]
    joined = jnp.concatenate([part[:, :columns] for part in weights], axis=0)
    for z in range(4):
        rows = jnp.concatenate([tokens[e, z] for e in range(tokens.shape[0])], axis=0)
        out[z] = dot(rows, joined).astype(BF16)


def total_kernel(capacity, place, low, high, *refs):
    sums, outs, whole = refs[:4], refs[4:8], refs[8]
    half = 2 * capacity
    whole[:half] = low[...] + sums[0][...].astype(F32) + sums[1][...].astype(F32)
    whole[half:] = high[...] + sums[2][...].astype(F32) + sums[3][...].astype(F32)
    for k, out in enumerate(outs):
        for j in range(4):

            @pl.when(place[k] == j)
            def _(out=out, j=j):
                out[...] = whole[j * capacity : (j + 1) * capacity].astype(out.dtype)


def unpack_kernel(capacity, arrived, low, high, tokens, rows, share):
    half = low.shape[0] // capacity
    for first, out in ((0, low), (half, high)):
        for k in range(half):
            block = arrived[first + k].astype(F32)
            rows[k * capacity : (k + 1) * capacity] = block[:capacity]
        out[...] = rows[...].astype(BF16)
    width = tokens.shape[3]
    for z in range(tokens.shape[1]):
        block = arrived[z].astype(F32)
        for r in range(tokens.shape[2] // 4):
            for j in range(4):
                share[4 * r + j : 4 * r + j + 1] = block[
                    capacity + r : capacity + r + 1, j * width : (j + 1) * width
                ]
        value = share[...].astype(BF16)
        for e in range(tokens.shape[0]):
            tokens[e, z] = value


def in_line_order(parts, axis):
    order = (lax.axis_index(axis) - jnp.arange(4, dtype=jnp.int32)) % 4
    return jnp.stack(parts).at[order].get(mode="promise_in_bounds")


def dense_out_kernel(columns, place, act, *refs):
    weights, out = refs[:4], refs[4]
    contract = (((1,), (1,)), ((), ()))
    for k in range(4):
        part = lax.dot_general(
            act[...], weights[k][:, columns:], contract, preferred_element_type=F32
        ).astype(BF16)
        half = part.shape[0] // 8
        for side in range(2):
            pieces = [part[(2 * j + side) * half : (2 * j + side + 1) * half] for j in range(4)]
            out[2 * place[k] + side] = jnp.concatenate(pieces, axis=0)


def body(
    normed,
    residual,
    expert_index,
    pick_weight,
    dense_gate,
    dense_up,
    dense_down,
    expert_gate,
    expert_up,
    expert_down,
):
    tokens = normed[0]
    picks = expert_index[0]
    weights = pick_weight[0]
    tok_rows, width = tokens.shape
    n_expert = 8
    capacity = min(tok_rows, 9 * tok_rows // (4 * n_expert))
    core = lax.axis_index("core")
    mine = lax.axis_index("x") * 2 + core
    hidden = dense_gate.shape[2]
    slab = width // 4
    step = dense_gate.shape[1]
    piece = width // n_expert

    with jax.named_scope("dispatch"):
        slot = slots_of(picks, n_expert)
        is_mine = picks == mine
        positions = jnp.arange(capacity, dtype=jnp.int32)
        select = jnp.any(
            (positions[:, None, None] == slot[None, :, :]) & is_mine[None, :, :], axis=2
        ).astype(BF16)
        routed = dot(select, tokens).astype(BF16)

    with jax.named_scope("dense_weights"):
        stacked = jnp.concatenate([dense_gate[0], dense_up[0], dense_down[0]], axis=1)
        stacked = after(stacked, routed)
        slabs = [stacked] + [shifted(stacked, "y", by) for by in (1, 2, 3)]
        steps_back = jnp.arange(4, dtype=jnp.int32)
        place_y, place_z = ((lax.axis_index(axis) - steps_back) % 4 for axis in ("y", "z"))

    with jax.named_scope("combine"):
        target = picks * capacity + slot
        columns = jnp.arange(n_expert * capacity, dtype=jnp.int32)
        chosen = jnp.where(columns[None, None, :] == target[:, :, None], weights[:, :, None], 0.0)
        combine = jnp.sum(chosen, axis=1)
        coarse = lax.reduce_precision(combine, 8, 7)
        fine = lax.reduce_precision(combine - coarse, 8, 7)
        coarse, fine = coarse.astype(BF16), fine.astype(BF16)

    down = expert_down[0, 0]
    blank = jnp.zeros((width, -down.shape[0] % 256), BF16)
    gate_up = jnp.concatenate([expert_gate[0, 0], blank, expert_up[0, 0], blank], axis=1)

    half = 2 * capacity
    with jax.named_scope("rows_z"):
        share = tok_rows // n_expert
        own_share = lax.dynamic_slice_in_dim(tokens, mine * share, share, axis=0)
        own_share = own_share.reshape(share, 4, 4, step)
        own_share = own_share.at[:, place_y].get(mode="promise_in_bounds").transpose(2, 0, 1, 3)
        sent = [repeated(routed, 4), own_share.reshape(4, share // 4, width)]
        arrived = exchanged(jnp.concatenate(sent, axis=1), "z")
        coarse, fine, gate_up = after((coarse, fine, gate_up), routed)
        low, high, line_tokens = local_call(
            functools.partial(unpack_kernel, capacity),
            [jax.ShapeDtypeStruct((half, width), BF16)] * 2
            + [jax.ShapeDtypeStruct((n_expert, 4, share, slab), BF16)],
            scratch_shapes=[pltpu.VMEM((half, width), F32), pltpu.VMEM((share, slab), F32)],
        )(after(arrived, coarse, fine, gate_up, *slabs[1:]))

    with jax.named_scope("rows_y"):
        prev_low, next_low = shifted(low, "y", 1), shifted(low, "y", -1)
        far_low = shifted(prev_low, "y", 1)
        next_high, prev_high = shifted(high, "y", -1), shifted(high, "y", 1)
        far_high = shifted(next_high, "y", -1)

    with jax.named_scope("dense_tokens"):
        line_tokens = exchanged(line_tokens, EXPERT_AXES)
        pre = local_call(
            functools.partial(dense_in_kernel, 2 * hidden),
            jax.ShapeDtypeStruct((4, tok_rows, 2 * hidden), BF16),
        )(line_tokens, *slabs)

    half_bf16, half_f32 = (jax.ShapeDtypeStruct(low.shape, dtype) for dtype in (BF16, F32))
    in_smem, in_vmem = (pl.BlockSpec(memory_space=space) for space in (pltpu.SMEM, pltpu.VMEM))
    with jax.named_scope("experts"):
        relay_next, relay_prev, early_next, early_prev, next_part, prev_part = local_call(
            rows_kernel, [half_bf16] * 4 + [half_f32] * 2, LONG
        )(gate_up, down, far_low, far_high, next_high, prev_low, next_low, prev_high)

    with jax.named_scope("partials_y"):
        relay_next, relay_prev = shifted(relay_next, "y", 1), shifted(relay_prev, "y", -1)
    with jax.named_scope("dense_hidden"):
        pre = exchanged(pre, "z")
        pre = jnp.sum(pre.astype(F32), axis=0)
        act = swiglu(pre[:, :hidden], pre[:, hidden:])
        line_act = jnp.broadcast_to(act[None], (4,) + act.shape)
    with jax.named_scope("dense_out"):
        half_tokens = tok_rows // 2
        every_act = exchanged(line_act, "z").reshape(4 * tok_rows, hidden)
        by_block = local_call(
            functools.partial(dense_out_kernel, 2 * hidden),
            jax.ShapeDtypeStruct((n_expert, 4 * half_tokens, step), BF16),
            in_specs=[in_smem] + [in_vmem] * 5,
        )(place_y, every_act, *slabs)

    with jax.named_scope("partials_y"):
        early_next, early_prev = shifted(early_next, "y", 1), shifted(early_prev, "y", -1)
        relay_next, relay_prev = after((relay_next, relay_prev), line_act)
        late_next = (next_part + relay_next.astype(F32)).astype(BF16)
        late_prev = (prev_part + relay_prev.astype(F32)).astype(BF16)
        late_next, late_prev = after((late_next, late_prev))
        own_low, own_high = local_call(rows_kernel, [half_f32] * 2)(
            after(gate_up, late_next, late_prev), down, low, high
        )
        late_next, late_prev = shifted(late_next, "y", 1), shifted(late_prev, "y", -1)

    with jax.named_scope("partials_z"):
        rows_f32, rows_bf16 = (jax.ShapeDtypeStruct(routed.shape, dtype) for dtype in (F32, BF16))
        kept_rows, *sent = local_call(
            functools.partial(total_kernel, capacity),
            [rows_f32] + [rows_bf16] * 3,
            in_specs=[in_smem] + [in_vmem] * 6,
            scratch_shapes=[pltpu.VMEM((4 * capacity, width), F32)],
        )(place_z, after(own_low, by_block), own_high, late_next, early_prev, early_next, late_prev)
        recv = [shifted(sent[k], "z", -1 - k) for k in (1, 2, 0)]
        expert_out = (kept_rows + sum(part.astype(F32) for part in recv)).astype(BF16)

    with jax.named_scope("dense_out"):
        block_sum = jnp.sum(exchanged(by_block, EXPERT_AXES).astype(F32), axis=0).astype(BF16)
        block_sum = block_sum.reshape(4, half_tokens, step)
        blocks = []
        for by in range(4):
            there = (lax.axis_index("z") + by) % 4
            block = lax.dynamic_index_in_dim(block_sum, there, 0, keepdims=False)
            blocks.append(shifted(block, "z", by) if by else block)
        blocks = in_line_order(blocks, "z")
        kept = lax.dynamic_slice_in_dim(blocks, 2 * core, 2, axis=0)
        given = lax.dynamic_slice_in_dim(blocks, 2 - 2 * core, 2, axis=0)
        taken = shifted(given, "core", 1)
        first = jnp.where(core == 0, kept, taken)
        second = jnp.where(core == 0, taken, kept)
        dense_total = jnp.concatenate([first, second], axis=1).transpose(1, 0, 2)
    base = residual[0].astype(F32) + dense_total.reshape(tok_rows, piece).astype(F32)

    with jax.named_scope("combine"):
        by_feature = expert_out.reshape(capacity, n_expert, piece).transpose(1, 0, 2)
        returned = exchanged(by_feature, EXPERT_AXES).reshape(n_expert * capacity, piece)
        spread = dot(coarse, returned) + dot(fine, returned)
        mixed = (base + spread).astype(BF16)
    with jax.named_scope("next_section"):
        return shifted(mixed, "section", 1)[None]


def solution(mesh):
    fine_mesh = Mesh(mesh.devices.reshape(GRID), AXES)
    data = ("y", "z")
    placed = (
        P("section", data, None),
        P("section", data, EXPERT_AXES),
        P("section", data, None),
        P("section", data, None),
        P("section", data, EXPERT_AXES),
        P("section", data, EXPERT_AXES),
        P("section", data, EXPERT_AXES),
        P("section", EXPERT_AXES, None, data),
        P("section", EXPERT_AXES, None, data),
        P("section", EXPERT_AXES, data, None),
    )
    return jax.shard_map(
        body,
        mesh=fine_mesh,
        in_specs=placed,
        out_specs=P("section", data, EXPERT_AXES),
        check_vma=False,
    )
```

```python
import functools

import jax
import jax.numpy as jnp
from jax import lax
from jax.experimental import pallas as pl
from jax.experimental.pallas import tpu as pltpu
from jax.sharding import Mesh, PartitionSpec as P

AXES = ("section", "y", "z", "x", "core")
GRID = (4, 4, 4, 4, 2)
EXPERT_AXES = ("x", "core")
BF16, F32 = jnp.bfloat16, jnp.float32
LONG = 100 * 1024**3


def shifted(x, axis, by):
    peers = lax.axis_size(axis)
    return lax.ppermute(x, axis, [(i, (i + by) % peers) for i in range(peers)])


def exchanged(x, axes):
    return lax.all_to_all(x, axes, split_axis=0, concat_axis=0, tiled=True)


def repeated(x, times):
    return jnp.broadcast_to(x[None], (times,) + x.shape)


def after(x, *others):
    return lax.optimization_barrier((x,) + others)[0]


def swiglu(first, second):
    return (jax.nn.silu(first) * second).astype(BF16)


def dot(a, b):
    return jnp.dot(a, b, preferred_element_type=F32)


def slots_of(picks, n_expert):
    labels = jnp.arange(n_expert, dtype=jnp.int32)
    named = (picks[:, :, None] == labels[None, None, :]).astype(jnp.int32)
    per_token = jnp.sum(named, axis=1, dtype=jnp.int32)
    earlier = jnp.cumsum(per_token, axis=0, dtype=jnp.int32) - per_token
    return jnp.sum(named * earlier[:, None, :], axis=2, dtype=jnp.int32)


def local_call(kernel, out_shape, flops=2 * 1024**3, **kwargs):
    return pl.pallas_call(
        kernel,
        out_shape=out_shape,
        compiler_params=pltpu.CompilerParams(vmem_limit_bytes=52 * 1024 * 1024),
        cost_estimate=pl.CostEstimate(
            flops=flops, bytes_accessed=4 * 1024**2, transcendentals=0
        ),
        **kwargs,
    )


def expert_rows(parts, gate_up, down):
    inner = down.shape[0]
    rows = jnp.concatenate([part[...].astype(F32) for part in parts], axis=0).astype(BF16)
    both = dot(rows, gate_up[...])
    start = both.shape[1] // 2
    first, second = both[:, :inner], both[:, start : start + inner]
    return dot((first / (1.0 + jnp.exp(-first)) * second).astype(BF16), down[...])


def rows_kernel(gate_up, down, *refs):
    parts, outs = refs[: len(refs) // 2], refs[len(refs) // 2 :]
    result = expert_rows(parts, gate_up, down)
    size = parts[0].shape[0]
    for k, out in enumerate(outs):
        out[...] = result[k * size : (k + 1) * size].astype(out.dtype)


def dense_in_kernel(columns, tokens, *refs):
    weights, out = refs[:4], refs[4]
    joined = jnp.concatenate([part[:, :columns] for part in weights], axis=0)
    for z in range(4):
        rows = jnp.concatenate([tokens[e, z] for e in range(tokens.shape[0])], axis=0)
        out[z] = dot(rows, joined).astype(BF16)


def total_kernel(capacity, place, low, high, *refs):
    sums, outs, whole = refs[:4], refs[4:8], refs[8]
    half = 2 * capacity
    whole[:half] = low[...] + sums[0][...].astype(F32) + sums[1][...].astype(F32)
    whole[half:] = high[...] + sums[2][...].astype(F32) + sums[3][...].astype(F32)
    for k, out in enumerate(outs):
        for j in range(4):

            @pl.when(place[k] == j)
            def _(out=out, j=j):
                out[...] = whole[j * capacity : (j + 1) * capacity].astype(out.dtype)


def unpack_kernel(capacity, arrived, low, high, tokens, rows, share):
    half = low.shape[0] // capacity
    for first, out in ((0, low), (half, high)):
        for k in range(half):
            block = arrived[first + k].astype(F32)
            rows[k * capacity : (k + 1) * capacity] = block[:capacity]
        out[...] = rows[...].astype(BF16)
    width = tokens.shape[3]
    for z in range(tokens.shape[1]):
        block = arrived[z].astype(F32)
        for r in range(tokens.shape[2] // 4):
            for j in range(4):
                share[4 * r + j : 4 * r + j + 1] = block[
                    capacity + r : capacity + r + 1, j * width : (j + 1) * width
                ]
        value = share[...].astype(BF16)
        for e in range(tokens.shape[0]):
            tokens[e, z] = value


def in_line_order(parts, axis):
    order = (lax.axis_index(axis) - jnp.arange(4, dtype=jnp.int32)) % 4
    return jnp.stack(parts).at[order].get(mode="promise_in_bounds")


def dense_out_kernel(columns, place, act, *refs):
    weights, out = refs[:4], refs[4]
    size = out.shape[2] // 4
    starts = [(2 * j + side) * size for side in range(2) for j in range(4)]
    tokens = jnp.concatenate([act[start : start + size] for start in starts], axis=0)
    contract = (((1,), (1,)), ((), ()))
    for k in range(4):
        part = lax.dot_general(
            weights[k][:, columns:], tokens, contract, preferred_element_type=F32
        ).astype(BF16)
        for side in range(2):
            out[2 * place[k] + side] = part[:, side * 4 * size : (side + 1) * 4 * size]


def body(
    normed,
    residual,
    expert_index,
    pick_weight,
    dense_gate,
    dense_up,
    dense_down,
    expert_gate,
    expert_up,
    expert_down,
):
    tokens = normed[0]
    picks = expert_index[0]
    weights = pick_weight[0]
    tok_rows, width = tokens.shape
    n_expert = 8
    capacity = min(tok_rows, 9 * tok_rows // (4 * n_expert))
    core = lax.axis_index("core")
    mine = lax.axis_index("x") * 2 + core
    hidden = dense_gate.shape[2]
    slab = width // 4
    step = dense_gate.shape[1]
    piece = width // n_expert

    with jax.named_scope("dispatch"):
        slot = slots_of(picks, n_expert)
        is_mine = picks == mine
        positions = jnp.arange(capacity, dtype=jnp.int32)
        select = jnp.any(
            (positions[:, None, None] == slot[None, :, :]) & is_mine[None, :, :], axis=2
        ).astype(BF16)
        routed = dot(select, tokens).astype(BF16)

    with jax.named_scope("dense_weights"):
        stacked = jnp.concatenate([dense_gate[0], dense_up[0], dense_down[0]], axis=1)
        stacked = after(stacked, routed)
        slabs = [stacked] + [shifted(stacked, "y", by) for by in (1, 2, 3)]
        steps_back = jnp.arange(4, dtype=jnp.int32)
        place_y, place_z = ((lax.axis_index(axis) - steps_back) % 4 for axis in ("y", "z"))

    with jax.named_scope("combine"):
        target = picks * capacity + slot
        columns = jnp.arange(n_expert * capacity, dtype=jnp.int32)
        chosen = jnp.where(columns[None, None, :] == target[:, :, None], weights[:, :, None], 0.0)
        combine = jnp.sum(chosen, axis=1)
        coarse = lax.reduce_precision(combine, 8, 7)
        fine = lax.reduce_precision(combine - coarse, 8, 7)
        coarse, fine = coarse.astype(BF16), fine.astype(BF16)

    down = expert_down[0, 0]
    blank = jnp.zeros((width, -down.shape[0] % 256), BF16)
    gate_up = jnp.concatenate([expert_gate[0, 0], blank, expert_up[0, 0], blank], axis=1)

    half = 2 * capacity
    with jax.named_scope("rows_z"):
        share = tok_rows // n_expert
        own_share = lax.dynamic_slice_in_dim(tokens, mine * share, share, axis=0)
        own_share = own_share.reshape(share, 4, 4, step)
        own_share = own_share.at[:, place_y].get(mode="promise_in_bounds").transpose(2, 0, 1, 3)
        sent = [repeated(routed, 4), own_share.reshape(4, share // 4, width)]
        arrived = exchanged(jnp.concatenate(sent, axis=1), "z")
        coarse, fine, gate_up = after((coarse, fine, gate_up), routed)
        low, high, line_tokens = local_call(
            functools.partial(unpack_kernel, capacity),
            [jax.ShapeDtypeStruct((half, width), BF16)] * 2
            + [jax.ShapeDtypeStruct((n_expert, 4, share, slab), BF16)],
            scratch_shapes=[pltpu.VMEM((half, width), F32), pltpu.VMEM((share, slab), F32)],
        )(after(arrived, coarse, fine, gate_up, *slabs[1:]))

    with jax.named_scope("rows_y"):
        prev_low, next_low = shifted(low, "y", 1), shifted(low, "y", -1)
        far_low = shifted(prev_low, "y", 1)
        next_high, prev_high = shifted(high, "y", -1), shifted(high, "y", 1)
        far_high = shifted(next_high, "y", -1)

    with jax.named_scope("dense_tokens"):
        line_tokens = exchanged(line_tokens, EXPERT_AXES)
        pre = local_call(
            functools.partial(dense_in_kernel, 2 * hidden),
            jax.ShapeDtypeStruct((4, tok_rows, 2 * hidden), BF16),
        )(line_tokens, *slabs)

    half_bf16, half_f32 = (jax.ShapeDtypeStruct(low.shape, dtype) for dtype in (BF16, F32))
    in_smem, in_vmem = (pl.BlockSpec(memory_space=space) for space in (pltpu.SMEM, pltpu.VMEM))
    with jax.named_scope("experts"):
        relay_next, relay_prev, early_next, early_prev, next_part, prev_part = local_call(
            rows_kernel, [half_bf16] * 6, LONG
        )(gate_up, down, far_low, far_high, next_high, prev_low, next_low, prev_high)

    with jax.named_scope("partials_y"):
        relay_next, relay_prev = shifted(relay_next, "y", 1), shifted(relay_prev, "y", -1)
    with jax.named_scope("dense_hidden"):
        pre = exchanged(pre, "z")
        pre = jnp.sum(pre.astype(F32), axis=0)
        act = swiglu(pre[:, :hidden], pre[:, hidden:])
        line_act = jnp.broadcast_to(act[None], (4,) + act.shape)
    with jax.named_scope("dense_out"):
        half_tokens = tok_rows // 2
        every_act = exchanged(line_act, "z").reshape(4 * tok_rows, hidden)
        by_block = local_call(
            functools.partial(dense_out_kernel, 2 * hidden),
            jax.ShapeDtypeStruct((n_expert, step, 4 * half_tokens), BF16),
            in_specs=[in_smem] + [in_vmem] * 5,
        )(place_y, every_act, *slabs)

    with jax.named_scope("partials_y"):
        early_next, early_prev = shifted(early_next, "y", 1), shifted(early_prev, "y", -1)
        relay_next, relay_prev = after((relay_next, relay_prev), line_act)
        late_next = (next_part.astype(F32) + relay_next.astype(F32)).astype(BF16)
        late_prev = (prev_part.astype(F32) + relay_prev.astype(F32)).astype(BF16)
        late_next, late_prev = after((late_next, late_prev))
        own_low, own_high = local_call(rows_kernel, [half_f32] * 2)(
            after(gate_up, late_next, late_prev), down, low, high
        )
        late_next, late_prev = shifted(late_next, "y", 1), shifted(late_prev, "y", -1)

    with jax.named_scope("partials_z"):
        rows_f32, rows_bf16 = (jax.ShapeDtypeStruct(routed.shape, dtype) for dtype in (F32, BF16))
        kept_rows, *sent = local_call(
            functools.partial(total_kernel, capacity),
            [rows_f32] + [rows_bf16] * 3,
            in_specs=[in_smem] + [in_vmem] * 6,
            scratch_shapes=[pltpu.VMEM((4 * capacity, width), F32)],
        )(place_z, after(own_low, by_block), own_high, late_next, early_prev, early_next, late_prev)
        recv = [shifted(sent[k], "z", -1 - k) for k in (1, 2, 0)]
        expert_out = (kept_rows + sum(part.astype(F32) for part in recv)).astype(BF16)

    with jax.named_scope("dense_out"):
        block_sum = jnp.sum(exchanged(by_block, EXPERT_AXES).astype(F32), axis=0).astype(BF16)
        block_sum = block_sum.T.reshape(4, half_tokens, step)
        blocks = []
        for by in range(4):
            there = (lax.axis_index("z") + by) % 4
            block = lax.dynamic_index_in_dim(block_sum, there, 0, keepdims=False)
            blocks.append(shifted(block, "z", by) if by else block)
        blocks = in_line_order(blocks, "z")
        kept = lax.dynamic_slice_in_dim(blocks, 2 * core, 2, axis=0)
        given = lax.dynamic_slice_in_dim(blocks, 2 - 2 * core, 2, axis=0)
        taken = shifted(given, "core", 1)
        first = jnp.where(core == 0, kept, taken)
        second = jnp.where(core == 0, taken, kept)
        dense_total = jnp.concatenate([first, second], axis=1).transpose(1, 0, 2)
    base = residual[0].astype(F32) + dense_total.reshape(tok_rows, piece).astype(F32)

    with jax.named_scope("combine"):
        by_feature = expert_out.reshape(capacity, n_expert, piece).transpose(1, 0, 2)
        returned = exchanged(by_feature, EXPERT_AXES).reshape(n_expert * capacity, piece)
        spread = dot(coarse, returned) + dot(fine, returned)
        mixed = (base + spread).astype(BF16)
    with jax.named_scope("next_section"):
        return shifted(mixed, "section", 1)[None]


def solution(mesh):
    fine_mesh = Mesh(mesh.devices.reshape(GRID), AXES)
    data = ("y", "z")
    placed = (
        P("section", data, None),
        P("section", data, EXPERT_AXES),
        P("section", data, None),
        P("section", data, None),
        P("section", data, EXPERT_AXES),
        P("section", data, EXPERT_AXES),
        P("section", data, EXPERT_AXES),
        P("section", EXPERT_AXES, None, data),
        P("section", EXPERT_AXES, None, data),
        P("section", EXPERT_AXES, data, None),
    )
    return jax.shard_map(
        body,
        mesh=fine_mesh,
        in_specs=placed,
        out_specs=P("section", data, EXPERT_AXES),
        check_vma=False,
    )
```
